128 devices in a mesh: group: 4 (over z_lo, core), tp: 32 (over y, z_hi, x).
Axes of the slice: x: 4, y: 4, z: 4 (z_hi: 2, z_lo: 2; z = z_hi * 2 + z_lo), core: 2. Of those that a mesh axis runs over, the one named last changes fastest.
Arguments:
- hidden_states: bfloat16 [4, 768, 8192], P(None, ('group', 'tp')), may hold values from -400 to 400
- norm_gain: bfloat16 [8192], replicated, may hold values from 0.099609375 to 1.8984375
- lengths: int32 [768], P(('group', 'tp')), may hold values from 2 to 512, as said below
- rotated_key_cache: bfloat16 [768, 512, 1024], P(('group', 'tp')), may hold values from -80 to 80
- value_cache: bfloat16 [768, 512, 1024], P(('group', 'tp')), may hold values from -8 to 8
- qkv_weight: bfloat16 [8192, 10240], P(('group', 'tp')), may hold values from -0.0625 to 0.0625
- qkv_grad: bfloat16 [8192, 10240], P(('group', 'tp')), may hold values from -6 to 6
- qkv_first: bfloat16 [8192, 10240], P(('group', 'tp')), may hold values from -0.59765625 to 0.59765625
- qkv_second: bfloat16 [8192, 10240], P(('group', 'tp')), may hold values from 0.0049743652 to 0.19921875
- out_weight: bfloat16 [8192, 8192], P(('group', 'tp')), may hold values from -0.0625 to 0.0625
- out_grad: bfloat16 [8192, 8192], P(('group', 'tp')), may hold values from -6 to 6
- out_first: bfloat16 [8192, 8192], P(('group', 'tp')), may hold values from -0.59765625 to 0.59765625
- out_second: bfloat16 [8192, 8192], P(('group', 'tp')), may hold values from 0.0049743652 to 0.19921875
Outputs:
- layer_out: bfloat16 [4, 768, 8192], P(None, 'group', 'tp')
The draws below stay inside these ranges and needn't reach their ends.
Inputs may be any that keep to these rules, and one draw needn't show every extreme that they name: `lengths`: in each aligned block of 6 rows one row has length 512.
All inputs are finite; a program needn't handle non-finite values.
Results may differ from the reference program's by a relative error of at most 0.011.
The reference program's roundings to bfloat16 on the way count: a program that leaves them out, or rounds other values in their place, can miss the bound.
Values may be sent and summed in bfloat16 or wider, within the bound.
No kernel may reach another device: no remote copies, remote signals or barrier semaphores. Data moves between devices by JAX's collectives and lax.ppermute only.
A program may use at most 192 MiB of HBM per device.

```python
import math
import jax
import jax.numpy as jnp
from jax import lax

D = 8192
HQ = 64
KEY_HEADS = 8
HEAD_SIZE = 128
LOCAL_ROWS = 6
CONTEXT_SLOTS = 512
DECODE_STEPS = 4
QUERY_WIDTH = 8192
KEY_WIDTH = 1024
QKV = 10240
TOTAL_BATCH = 768


def draw_hidden_states(key, part):
    key = jax.random.fold_in(key, 11)
    key_noise, key_rows, key_columns = jax.random.split(key, 3)
    row_scale = jnp.exp(jax.random.uniform(key_rows, (DECODE_STEPS, TOTAL_BATCH, 1), jnp.float32) * math.log(10.0))
    col_scale = jnp.exp(jax.random.uniform(key_columns, (1, 1, D), jnp.float32) * math.log(10.0))
    values_raw = jax.random.normal(key_noise, (DECODE_STEPS, TOTAL_BATCH, D), jnp.float32)
    values_raw = jnp.clip(values_raw, -4.0, 4.0)
    return (values_raw * row_scale * col_scale).astype(jnp.bfloat16)


def draw_lengths(key, part):
    key = jax.random.fold_in(key, 37)
    key_len, key_shift, key_pick = jax.random.split(key, 3)
    drawn_raw = jax.random.randint(key_len, (TOTAL_BATCH,), 2, CONTEXT_SLOTS + 1)
    shift_bits = jax.random.randint(key_shift, (TOTAL_BATCH,), 0, 6)
    shortened = jnp.maximum(jnp.right_shift(drawn_raw, shift_bits), 2)
    chosen_slot = jax.random.randint(key_pick, (TOTAL_BATCH // LOCAL_ROWS, 1), 0, LOCAL_ROWS)
    slot_index = jnp.arange(LOCAL_ROWS)[None, :]
    longest = (slot_index == chosen_slot).reshape(TOTAL_BATCH)
    return jnp.where(longest, CONTEXT_SLOTS, shortened).astype(jnp.int32)


def draw_rotated_key_cache(key, part):
    key = jax.random.fold_in(key, 23)
    key_base = jax.random.fold_in(key, 0)
    base_keys = jnp.clip(jax.random.normal(key_base, (TOTAL_BATCH, CONTEXT_SLOTS, KEY_WIDTH), jnp.float32), -4.0, 4.0)
    return base_keys.astype(jnp.bfloat16)


def steps_of(own_key, shape, cuts, least, largest):
    gain, own = 1.0, jax.random.fold_in(own_key, 6)
    for dim, parts in cuts:
        steps = jnp.exp(jax.random.uniform(jax.random.fold_in(own, dim), (parts,), jnp.float32, least / len(cuts), largest / len(cuts)))
        gain = gain * jnp.repeat(steps, shape[dim] // parts).reshape([-1 if axis == dim else 1 for axis in range(len(shape))])
    return gain


def gaussian(stream_key, extent, scale, bound, shards=(), kind=jnp.bfloat16):
    array = scale * jax.random.normal(stream_key, extent, jnp.float32)
    if shards:
        array = array * steps_of(stream_key, extent, shards, -0.22, 0.18)
    return jnp.clip(array, -bound, bound).astype(kind)


def setup_inputs(seed: int = 0) -> dict:
    streams_of = jax.random.split(jax.random.key(seed), 14)
    return {
        "hidden_states": draw_hidden_states(jax.random.fold_in(streams_of[13], 71), 0),
        "norm_gain": jnp.clip(1.0 + 0.18 * jax.random.normal(streams_of[1], (D,), jnp.float32), 0.099609375, 1.8984375).astype(jnp.bfloat16),
        "lengths": draw_lengths(jax.random.fold_in(streams_of[13], 71), 0),
        "rotated_key_cache": draw_rotated_key_cache(jax.random.fold_in(streams_of[13], 71), 0),
        "value_cache": gaussian(streams_of[4], (TOTAL_BATCH, CONTEXT_SLOTS, KEY_WIDTH), 2.0, 8.0, ((0, 128),)),
        "qkv_weight": gaussian(streams_of[5], (D, QKV), D ** -0.5, 0.0625, ((0, 128),)),
        "qkv_grad": gaussian(streams_of[6], (D, QKV), 1.0, 6.0, ((0, 128),)),
        "qkv_first": gaussian(streams_of[7], (D, QKV), 0.1, 0.59765625, ((0, 128),)),
        "qkv_second": jnp.clip(jnp.exp(math.log(0.19921875) - 3.6901057 * jax.random.uniform(streams_of[8], (D, QKV), jnp.float32) ** steps_of(streams_of[8], (D, QKV), ((0, 128),), -0.2, 0.2)), 0.0049743652, 0.19921875).astype(jnp.bfloat16),
        "out_weight": gaussian(streams_of[9], (QUERY_WIDTH, D), QUERY_WIDTH ** -0.5, 0.0625, ((0, 128),)),
        "out_grad": gaussian(streams_of[10], (QUERY_WIDTH, D), 1.0, 6.0, ((0, 128),)),
        "out_first": gaussian(streams_of[11], (QUERY_WIDTH, D), 0.1, 0.59765625, ((0, 128),)),
        "out_second": jnp.clip(jnp.exp(math.log(0.19921875) - 3.6901057 * jax.random.uniform(streams_of[12], (QUERY_WIDTH, D), jnp.float32) ** steps_of(streams_of[12], (QUERY_WIDTH, D), ((0, 128),), -0.2, 0.2)), 0.0049743652, 0.19921875).astype(jnp.bfloat16),
    }


learn_rate = 0.008
beta_one = 0.9
beta_two = 0.95
bias_one = 1.0 - beta_one * beta_one
bias_two = 1.0 - beta_two * beta_two
adam_eps = 1e-08
decay_rate = 0.1
rope_base = 500000.0
norm_eps = 1e-05

def adam_step(weight, gradient, moment_one, moment_two):
    grad_wide = gradient.astype(jnp.float32)
    first_new = beta_one * moment_one.astype(jnp.float32) + (1.0 - beta_one) * grad_wide
    second_new = beta_two * moment_two.astype(jnp.float32) + (1.0 - beta_two) * grad_wide * grad_wide
    weight_wide = weight.astype(jnp.float32)
    update = first_new / bias_one / (jnp.sqrt(second_new / bias_two) + adam_eps) + decay_rate * weight_wide
    return (weight_wide - learn_rate * update).astype(jnp.bfloat16)

def rms_norm(rows_in, gain_vector):
    rows_wide = rows_in.astype(jnp.float32)
    inverse = lax.rsqrt(lax.optimization_barrier(jnp.mean(rows_wide * rows_wide, axis=-1, keepdims=True)) + norm_eps)
    return (rows_wide * inverse * gain_vector.astype(jnp.float32)).astype(jnp.bfloat16)

def apply_rotary(vectors, token_positions):
    half_width = vectors.shape[-1] // 2
    frequency = jnp.power(rope_base, -2.0 * jnp.arange(half_width, dtype=jnp.float32) / vectors.shape[-1])
    angles = token_positions.astype(jnp.float32)[..., None, None] * frequency
    cosine = jnp.cos(angles)
    sine_part = jnp.sin(angles)
    vectors_wide = vectors.astype(jnp.float32)
    lead_half = vectors_wide[..., :half_width]
    tail_half = vectors_wide[..., half_width:]
    return jnp.concatenate([lead_half * cosine - tail_half * sine_part, tail_half * cosine + lead_half * sine_part], axis=-1).astype(jnp.bfloat16)

def attend(queries, stored_keys, stored_values, fresh_keys, fresh_values, lengths, step_index):
    row_number, head_count, head_dim = queries.shape
    kv_heads = stored_keys.shape[2]
    grouped = queries.reshape(row_number, kv_heads, head_count // kv_heads, head_dim).astype(jnp.float32)
    score_scale = 1.0 / math.sqrt(head_dim)
    cache_scores = jnp.einsum('rkgd,rckd->rkgc', grouped, stored_keys.astype(jnp.float32)) * score_scale
    new_scores = jnp.einsum('rkgd,srkd->rkgs', grouped, fresh_keys.astype(jnp.float32)) * score_scale
    cache_live = jnp.arange(stored_keys.shape[1])[None, :] < lengths[:, None]
    new_live = jnp.arange(fresh_keys.shape[0]) <= step_index
    cache_scores = jnp.where(cache_live[:, None, None, :], cache_scores, -jnp.inf)
    new_scores = jnp.where(new_live, new_scores, -jnp.inf)
    highest = jnp.maximum(lax.optimization_barrier(jnp.max(cache_scores, axis=-1)), lax.optimization_barrier(jnp.max(new_scores, axis=-1)))[..., None]
    cache_exp = jnp.exp(cache_scores - highest)
    new_exp = jnp.exp(new_scores - highest)
    denominator = lax.optimization_barrier(jnp.sum(cache_exp, axis=-1, keepdims=True)) + lax.optimization_barrier(jnp.sum(new_exp, axis=-1, keepdims=True))
    cache_prob = (cache_exp / denominator).astype(jnp.bfloat16)
    new_prob = (new_exp / denominator).astype(jnp.bfloat16)
    attended = jnp.einsum('rkgc,rckd->rkgd', cache_prob.astype(jnp.float32), stored_values.astype(jnp.float32))
    attended = attended + jnp.einsum('rkgs,srkd->rkgd', new_prob.astype(jnp.float32), fresh_values.astype(jnp.float32))
    return attended.reshape(row_number, head_count * head_dim).astype(jnp.bfloat16)

def reference(hidden_states, norm_gain, lengths, rotated_key_cache, value_cache, qkv_weight, qkv_grad, qkv_first, qkv_second, out_weight, out_grad, out_first, out_second):
    qkv_updated = adam_step(qkv_weight, qkv_grad, qkv_first, qkv_second)
    out_updated = adam_step(out_weight, out_grad, out_first, out_second)
    block_number = TOTAL_BATCH // LOCAL_ROWS
    key_block_list = rotated_key_cache.reshape(block_number, LOCAL_ROWS, CONTEXT_SLOTS, KEY_HEADS, HEAD_SIZE)
    value_block_list = value_cache.reshape(block_number, LOCAL_ROWS, CONTEXT_SLOTS, KEY_HEADS, HEAD_SIZE)
    length_blocks = lengths.reshape(block_number, LOCAL_ROWS)
    fresh_keys = jnp.zeros((DECODE_STEPS, TOTAL_BATCH, KEY_HEADS, HEAD_SIZE), jnp.bfloat16)
    fresh_values = jnp.zeros((DECODE_STEPS, TOTAL_BATCH, KEY_HEADS, HEAD_SIZE), jnp.bfloat16)
    outputs = []
    for step_index in range(DECODE_STEPS):
        normed = rms_norm(hidden_states[step_index], norm_gain)
        projected_input = jnp.dot(normed, qkv_updated, preferred_element_type=jnp.float32).astype(jnp.bfloat16)
        token_positions = lengths + step_index
        queries = apply_rotary(projected_input[:, :QUERY_WIDTH].reshape(TOTAL_BATCH, HQ, HEAD_SIZE), token_positions)
        current_keys = apply_rotary(projected_input[:, QUERY_WIDTH:QUERY_WIDTH + KEY_WIDTH].reshape(TOTAL_BATCH, KEY_HEADS, HEAD_SIZE), token_positions)
        current_values = projected_input[:, QUERY_WIDTH + KEY_WIDTH:].reshape(TOTAL_BATCH, KEY_HEADS, HEAD_SIZE)
        fresh_keys = fresh_keys.at[step_index].set(current_keys)
        fresh_values = fresh_values.at[step_index].set(current_values)
        fresh_key_blocks = jnp.moveaxis(fresh_keys.reshape(DECODE_STEPS, block_number, LOCAL_ROWS, KEY_HEADS, HEAD_SIZE), 1, 0)
        fresh_value_blocks = jnp.moveaxis(fresh_values.reshape(DECODE_STEPS, block_number, LOCAL_ROWS, KEY_HEADS, HEAD_SIZE), 1, 0)

        def one_block(operands, step_index=step_index):
            block_q, block_k, block_v, block_nk, block_nv, block_len = operands
            return attend(block_q, block_k, block_v, block_nk, block_nv, block_len, step_index)
        attended = lax.map(one_block, (queries.reshape(block_number, LOCAL_ROWS, HQ, HEAD_SIZE), key_block_list, value_block_list, fresh_key_blocks, fresh_value_blocks, length_blocks))
        attended = attended.reshape(TOTAL_BATCH, QUERY_WIDTH)
        outputs.append(jnp.dot(attended, out_updated, preferred_element_type=jnp.float32).astype(jnp.bfloat16))
    return jnp.stack(outputs)
```

```python
import math

import jax
import jax.numpy as jnp
from jax import lax
from jax.sharding import PartitionSpec as P

D = 8192
HQ = 64
KEY_HEADS = 8
HEAD_SIZE = 128
CONTEXT_SLOTS = 512
DECODE_STEPS = 4
QUERY_WIDTH = 8192
KEY_WIDTH = 1024


learn_rate = 0.008
beta_one = 0.9
beta_two = 0.95
bias_one = 1.0 - beta_one * beta_one
bias_two = 1.0 - beta_two * beta_two
adam_eps = 1e-08
decay_rate = 0.1
rope_base = 500000.0
norm_eps = 1e-05


def adam_step(weight, gradient, moment_one, moment_two):
    grad_wide = gradient.astype(jnp.float32)
    first_new = beta_one * moment_one.astype(jnp.float32) + (1.0 - beta_one) * grad_wide
    second_new = (
        beta_two * moment_two.astype(jnp.float32) + (1.0 - beta_two) * grad_wide * grad_wide
    )
    weight_wide = weight.astype(jnp.float32)
    update = (
        first_new / bias_one / (jnp.sqrt(second_new / bias_two) + adam_eps)
        + decay_rate * weight_wide
    )
    return (weight_wide - learn_rate * update).astype(jnp.bfloat16)


def rms_norm(rows_in, gain_vector):
    rows_wide = rows_in.astype(jnp.float32)
    inverse = lax.rsqrt(jnp.mean(rows_wide * rows_wide, axis=-1, keepdims=True) + norm_eps)
    return (rows_wide * inverse * gain_vector.astype(jnp.float32)).astype(jnp.bfloat16)


def apply_rotary(vectors, token_positions):
    half_width = vectors.shape[-1] // 2
    frequency = jnp.power(
        rope_base, -2.0 * jnp.arange(half_width, dtype=jnp.float32) / vectors.shape[-1]
    )
    angles = token_positions.astype(jnp.float32)[..., None, None] * frequency
    cosine = jnp.cos(angles)
    sine_part = jnp.sin(angles)
    vectors_wide = vectors.astype(jnp.float32)
    lead_half = vectors_wide[..., :half_width]
    tail_half = vectors_wide[..., half_width:]
    return jnp.concatenate(
        [lead_half * cosine - tail_half * sine_part, tail_half * cosine + lead_half * sine_part],
        axis=-1,
    ).astype(jnp.bfloat16)


def unpack(fields, tp_count, token_positions):
    local_steps = fields.shape[0]
    row_number = fields.shape[1]
    block_list = fields.reshape(local_steps, row_number, tp_count, -1)
    query_columns = QUERY_WIDTH // tp_count
    key_columns = KEY_WIDTH // tp_count
    queries = apply_rotary(
        block_list[..., :query_columns].reshape(local_steps, row_number, HQ, HEAD_SIZE),
        token_positions,
    )
    current_keys = apply_rotary(
        block_list[..., query_columns : query_columns + key_columns].reshape(
            local_steps, row_number, KEY_HEADS, HEAD_SIZE
        ),
        token_positions,
    )
    current_values = block_list[..., query_columns + key_columns :].reshape(
        local_steps, row_number, KEY_HEADS, HEAD_SIZE
    )
    return (queries, current_keys, current_values)


def attend(queries, stored_keys, stored_values, fresh_keys, fresh_values, lengths):
    steps, row_number, head_count, head_dim = queries.shape
    kv_heads = stored_keys.shape[2]
    grouped = queries.reshape(steps, row_number, kv_heads, head_count // kv_heads, head_dim)
    score_scale = 1.0 / math.sqrt(head_dim)
    cache_scores = (
        jnp.einsum("trkgd,rckd->rktgc", grouped, stored_keys, preferred_element_type=jnp.float32)
        * score_scale
    )
    new_scores = (
        jnp.einsum("trkgd,srkd->rktgs", grouped, fresh_keys, preferred_element_type=jnp.float32)
        * score_scale
    )
    cache_live = jnp.arange(stored_keys.shape[1])[None, :] < lengths[:, None]
    new_live = jnp.arange(steps)[None, :] <= jnp.arange(steps)[:, None]
    cache_scores = jnp.where(cache_live[:, None, None, None, :], cache_scores, -jnp.inf)
    new_scores = jnp.where(new_live[None, None, :, None, :], new_scores, -jnp.inf)
    highest = jnp.maximum(jnp.max(cache_scores, axis=-1), jnp.max(new_scores, axis=-1))[..., None]
    cache_exp = jnp.exp(cache_scores - highest)
    new_exp = jnp.exp(new_scores - highest)
    denominator = jnp.sum(cache_exp, axis=-1, keepdims=True) + jnp.sum(
        new_exp, axis=-1, keepdims=True
    )
    cache_prob = (cache_exp / denominator).astype(jnp.bfloat16)
    new_prob = (new_exp / denominator).astype(jnp.bfloat16)
    attended = jnp.einsum(
        "rktgc,rckd->trkgd", cache_prob, stored_values, preferred_element_type=jnp.float32
    )
    attended = attended + jnp.einsum(
        "rktgs,srkd->trkgd", new_prob, fresh_values, preferred_element_type=jnp.float32
    )
    return attended.reshape(steps, row_number, head_count * head_dim).astype(jnp.bfloat16)


PLANE = ("c", "y", "x")
PLANE_SIZE = 32
Z_SIZE = 4


def shift_z(value, step):
    def position(z):
        return (z % 2) * 2 + (z // 2) % 2

    return lax.ppermute(
        value, ("zl", "zh"), [(position(z), position(z + step + Z_SIZE)) for z in range(Z_SIZE)]
    )


def gather_along_z(piece):
    half = piece.shape[0] // 2
    below = shift_z(piece, 1)
    above = shift_z(piece, -1)
    far_first = shift_z(below[:half], 1)
    far_second = shift_z(above[half:], -1)
    return [piece, above, far_first, far_second, below]


def features_by_plane(rows):
    lead = rows.shape[:-1]
    z_index = lax.axis_index("zh") * 2 + lax.axis_index("zl")
    blocks = rows.reshape(*lead, 2, 2, 4, 2, 256)
    nd = len(lead)
    blocks = blocks.transpose(*range(nd), nd + 3, nd, nd + 1, nd + 2, nd + 4)
    blocks = blocks.reshape(*lead, Z_SIZE, D // Z_SIZE)
    twice = jnp.concatenate([blocks, blocks], axis=-2)
    return lax.dynamic_slice_in_dim(twice, z_index, Z_SIZE, axis=nd).reshape(*lead, D)


def multiply(rows, weights):
    total = None
    start = 0
    for weight in weights:
        depth = weight.shape[0]
        term = jnp.dot(
            rows[:, start : start + depth], weight, preferred_element_type=jnp.float32
        )
        total = term if total is None else total + term
        start += depth
    return total.astype(jnp.bfloat16)


def body(
    hidden_states,
    norm_gain,
    lengths,
    rotated_key_cache,
    value_cache,
    qkv_weight,
    qkv_grad,
    qkv_first,
    qkv_second,
    out_weight,
    out_grad,
    out_first,
    out_second,
):
    row_number = hidden_states.shape[1]
    local = DECODE_STEPS * row_number
    depth = qkv_weight.shape[0]

    normed = features_by_plane(rms_norm(hidden_states, norm_gain)).reshape(local, D)
    normed_rows = lax.all_gather(normed, PLANE, axis=0, tiled=True)

    qkv_updated = adam_step(qkv_weight, qkv_grad, qkv_first, qkv_second)
    query_columns = QUERY_WIDTH // PLANE_SIZE
    key_columns = KEY_WIDTH // PLANE_SIZE
    qkv_piece = jnp.concatenate(
        [
            qkv_updated[:, :QUERY_WIDTH].reshape(depth, PLANE_SIZE, query_columns),
            qkv_updated[:, QUERY_WIDTH : QUERY_WIDTH + KEY_WIDTH].reshape(
                depth, PLANE_SIZE, key_columns
            ),
            qkv_updated[:, QUERY_WIDTH + KEY_WIDTH :].reshape(depth, PLANE_SIZE, key_columns),
        ],
        axis=2,
    ).transpose(1, 0, 2)
    qkv_plane = lax.all_to_all(qkv_piece, PLANE, split_axis=0, concat_axis=0, tiled=True)
    qkv_owned = gather_along_z(qkv_plane.reshape(PLANE_SIZE * depth, -1))

    out_updated = adam_step(out_weight, out_grad, out_first, out_second)
    out_piece = out_updated.reshape(depth, 4, 2, 4, 256).transpose(2, 1, 3, 0, 4)
    out_piece = out_piece.reshape(PLANE_SIZE, depth, 256)
    out_plane = lax.all_to_all(out_piece, PLANE, split_axis=0, concat_axis=0, tiled=True)
    out_owned = gather_along_z(out_plane.reshape(PLANE_SIZE * depth, -1))

    projected = multiply(normed_rows, qkv_owned).reshape(PLANE_SIZE, local, -1)
    fields = lax.all_to_all(projected, PLANE, split_axis=0, concat_axis=0, tiled=True)
    fields = fields.reshape(PLANE_SIZE, DECODE_STEPS, row_number, -1).transpose(1, 2, 0, 3)

    token_positions = lengths[None, :] + jnp.arange(DECODE_STEPS, dtype=jnp.int32)[:, None]
    queries, fresh_keys, fresh_values = unpack(fields, PLANE_SIZE, token_positions)
    stored_keys = rotated_key_cache.reshape(row_number, CONTEXT_SLOTS, KEY_HEADS, HEAD_SIZE)
    stored_values = value_cache.reshape(row_number, CONTEXT_SLOTS, KEY_HEADS, HEAD_SIZE)
    attended = attend(queries, stored_keys, stored_values, fresh_keys, fresh_values, lengths)

    attended = features_by_plane(attended).reshape(local, D)
    attended_rows = lax.all_gather(attended, PLANE, axis=0, tiled=True)
    result = multiply(attended_rows, out_owned)
    return place_output(result, row_number)


def place_output(result, row_number):
    blocks = result.reshape(2, 4, 4, DECODE_STEPS, row_number, 256)
    zh_index = lax.axis_index("zh")
    c_index = lax.axis_index("c")
    same = lax.dynamic_index_in_dim(blocks, zh_index, axis=0, keepdims=False)
    other = lax.dynamic_index_in_dim(blocks, 1 - zh_index, axis=0, keepdims=False)
    pairs = [(c, zh) for c in range(2) for zh in range(2)]
    same = lax.ppermute(same, ("c", "zh"), [(c * 2 + zh, zh * 2 + c) for c, zh in pairs])
    other = lax.ppermute(other, ("c", "zh"), [(c * 2 + zh, (1 - zh) * 2 + c) for c, zh in pairs])
    first = jnp.where(c_index == 0, same, other)
    second = jnp.where(c_index == 0, other, same)
    joined = jnp.stack([first, second], axis=1)
    return joined.transpose(3, 0, 1, 2, 4, 5).reshape(DECODE_STEPS, 32 * row_number, 256)


def solution(mesh):
    fine = jax.sharding.Mesh(mesh.devices.reshape(2, 2, 4, 2, 4), ("zl", "c", "y", "zh", "x"))
    every = ("zl", "c", "y", "zh", "x")
    return jax.shard_map(
        body,
        mesh=fine,
        in_specs=(
            P(None, every, None),
            P(),
            P(every),
            P(every, None, None),
            P(every, None, None),
        )
        + (P(every, None),) * 8,
        out_specs=P(None, ("zl", "c"), ("y", "zh", "x")),
        check_vma=False,
    )
```

```python
import functools
import math

import jax
import jax.numpy as jnp
from jax import lax
from jax.experimental import pallas as pl
from jax.experimental.pallas import tpu as pltpu
from jax.sharding import PartitionSpec as P

D = 8192
HQ = 64
KEY_HEADS = 8
HEAD_SIZE = 128
CONTEXT_SLOTS = 512
DECODE_STEPS = 4
QUERY_WIDTH = 8192
KEY_WIDTH = 1024


learn_rate = 0.008
beta_one = 0.9
beta_two = 0.95
bias_one = 1.0 - beta_one * beta_one
bias_two = 1.0 - beta_two * beta_two
adam_eps = 1e-08
decay_rate = 0.1
rope_base = 500000.0
norm_eps = 1e-05


def adam_step(weight, gradient, moment_one, moment_two):
    grad_wide = gradient.astype(jnp.float32)
    first_new = beta_one * moment_one.astype(jnp.float32) + (1.0 - beta_one) * grad_wide
    second_new = (
        beta_two * moment_two.astype(jnp.float32) + (1.0 - beta_two) * grad_wide * grad_wide
    )
    weight_wide = weight.astype(jnp.float32)
    update = (
        first_new / bias_one / (jnp.sqrt(second_new / bias_two) + adam_eps)
        + decay_rate * weight_wide
    )
    return (weight_wide - learn_rate * update).astype(jnp.bfloat16)


def rms_norm(rows_in, gain_vector):
    rows_wide = rows_in.astype(jnp.float32)
    inverse = lax.rsqrt(jnp.mean(rows_wide * rows_wide, axis=-1, keepdims=True) + norm_eps)
    return (rows_wide * inverse * gain_vector.astype(jnp.float32)).astype(jnp.bfloat16)


PAIRS = 3
CHUNKS = ((0, 3),)
Z_SIZE = 4


def shift_z(value, step):
    def position(z):
        return (z % 2) * 2 + (z // 2) % 2

    return lax.ppermute(
        value, ("zl", "zh"), [(position(z), position(z + step + Z_SIZE)) for z in range(Z_SIZE)]
    )


def shift(value, axis, step):
    return lax.ppermute(value, axis, [(i, (i + step) % 4) for i in range(4)])


def place(target, update, *start):
    return lax.dynamic_update_slice(target, update, start)


def gather_along(block, axis, index):
    ring = jnp.zeros((4,) + block.shape, block.dtype)
    zeros = (0,) * block.ndim
    ring = place(ring, block[None], index, *zeros)
    for step in (1, -1, 2):
        moved = shift(block, axis, step)
        ring = place(ring, moved[None], (index - step + 4) % 4, *zeros)
    return ring


def gather_plane(rows):
    m, k = rows.shape
    half = k // 2
    iy, ix = lax.axis_index("y"), lax.axis_index("x")
    everything = jnp.zeros((4, 4, m, k), rows.dtype)
    first = gather_along(rows[:, :half], "x", ix)
    second = gather_along(rows[:, half:], "y", iy)
    first_low, first_high = shift(first, "y", 1), shift(first, "y", -1)
    second_low, second_high = shift(second, "x", 1), shift(second, "x", -1)
    first_far = shift(first_low[:2], "y", 1), shift(first_high[2:], "y", -1)
    second_far = shift(second_low[:2], "x", 1), shift(second_high[2:], "x", -1)
    everything = place(everything, first[None], iy, 0, 0, 0)
    everything = place(everything, second[:, None], 0, ix, 0, half)
    everything = place(everything, first_low[None], (iy + 3) % 4, 0, 0, 0)
    everything = place(everything, first_high[None], (iy + 1) % 4, 0, 0, 0)
    everything = place(everything, second_low[:, None], 0, (ix + 3) % 4, 0, half)
    everything = place(everything, second_high[:, None], 0, (ix + 1) % 4, 0, half)
    everything = place(everything, first_far[0][None], (iy + 2) % 4, 0, 0, 0)
    everything = place(everything, first_far[1][None], (iy + 2) % 4, 2, 0, 0)
    everything = place(everything, second_far[0][:, None], 0, (ix + 2) % 4, 0, half)
    everything = place(everything, second_far[1][:, None], 2, (ix + 2) % 4, 0, half)
    return everything.reshape(16 * m, k)


def rotary_tables(lengths):
    half_width = HEAD_SIZE // 2
    frequency = jnp.power(
        rope_base, -2.0 * jnp.arange(half_width, dtype=jnp.float32) / HEAD_SIZE
    )
    positions = lengths[:, None] + jnp.arange(DECODE_STEPS, dtype=jnp.int32)[None, :]
    angles = positions.astype(jnp.float32)[..., None] * frequency
    cosine, sine = jnp.cos(angles), jnp.sin(angles)
    shape = (PAIRS, 8, HEAD_SIZE)
    return (
        jnp.concatenate([cosine, cosine], axis=-1).reshape(shape),
        jnp.concatenate([-sine, sine], axis=-1).reshape(shape),
    )


def attention_kernel(first_pair, lengths_ref, place_ref, field_ref, cos_ref, sin_ref, key_ref,
                     value_ref, out_ref):
    pair = first_pair + pl.program_id(0)
    cosine, sine = cos_ref[0], sin_ref[0]
    scale = 1.0 / math.sqrt(HEAD_SIZE)
    row = lax.broadcasted_iota(jnp.int32, (64, 1), 0)
    second_row = ((row >> 2) & 1) == 1
    step = row & 3
    length = jnp.where(second_row, lengths_ref[2 * pair + 1], lengths_ref[2 * pair])
    live = lax.broadcasted_iota(jnp.int32, (64, CONTEXT_SLOTS), 1) < length
    fresh_column = lax.broadcasted_iota(jnp.int32, (64, 8), 1)
    fresh_live = (((fresh_column >> 2) & 1) == ((row >> 2) & 1)) & ((fresh_column & 3) <= step)

    def field(block, start):
        y, x = block // 4, block % 4
        total = None
        for zl in range(2):
            for zh in range(2):
                source = zl * 32 + y * 8 + zh * 4 + x
                term = field_ref[source, 0, :, start : start + 128].astype(jnp.float32)
                total = term if total is None else total + term
        return total.astype(jnp.bfloat16).astype(jnp.float32)

    def rotate(vector):
        return vector * cosine + pltpu.roll(vector, 64, 1) * sine

    def times_transposed(left, right):
        return lax.dot_general(
            left, right, (((1,), (1,)), ((), ())), preferred_element_type=jnp.float32
        )

    for kv in range(KEY_HEADS):
        columns = slice(kv * HEAD_SIZE, (kv + 1) * HEAD_SIZE)
        query = jnp.concatenate(
            [rotate(field(2 * kv + h // 4, (h % 4) * 128)) for h in range(8)], axis=0
        ).astype(jnp.bfloat16)
        fresh_key = rotate(field(kv, 512)).astype(jnp.bfloat16)
        fresh_value = field(8 + kv, 512).astype(jnp.bfloat16)
        scores = jnp.where(
            second_row,
            times_transposed(query, key_ref[1, :, columns]),
            times_transposed(query, key_ref[0, :, columns]),
        ) * scale
        fresh_scores = times_transposed(query, fresh_key) * scale
        scores = jnp.where(live, scores, -jnp.inf)
        fresh_scores = jnp.where(fresh_live, fresh_scores, -jnp.inf)
        highest = jnp.maximum(
            jnp.max(scores, axis=-1, keepdims=True), jnp.max(fresh_scores, axis=-1, keepdims=True)
        )
        weight = jnp.exp(scores - highest)
        fresh_weight = jnp.exp(fresh_scores - highest)
        inverse = 1.0 / (
            jnp.sum(weight, axis=-1, keepdims=True) + jnp.sum(fresh_weight, axis=-1, keepdims=True)
        )
        prob = weight * inverse
        fresh_prob = (fresh_weight * inverse).astype(jnp.bfloat16)
        attended = (
            jnp.dot(
                jnp.where(second_row, 0.0, prob).astype(jnp.bfloat16),
                value_ref[0, :, columns],
                preferred_element_type=jnp.float32,
            )
            + jnp.dot(
                jnp.where(second_row, prob, 0.0).astype(jnp.bfloat16),
                value_ref[1, :, columns],
                preferred_element_type=jnp.float32,
            )
            + jnp.dot(fresh_prob, fresh_value, preferred_element_type=jnp.float32)
        )
        for h in range(8):
            start = pl.multiple_of(place_ref[4 * kv + h // 2] * 256 + (h % 2) * 128, 128)
            out_ref[0, :, pl.ds(start, 128)] = attended[8 * h : 8 * h + 8].astype(jnp.bfloat16)


def attention(fields, cosine, sine, keys, values, lengths, places, first_pair):
    pairs = fields.shape[1]
    table = pl.BlockSpec((1, 8, HEAD_SIZE), lambda i, *_: (first_pair + i, 0, 0))
    cache = pl.BlockSpec((2, CONTEXT_SLOTS, KEY_WIDTH), lambda i, *_: (first_pair + i, 0, 0))
    return pl.pallas_call(
        functools.partial(attention_kernel, first_pair),
        out_shape=jax.ShapeDtypeStruct((pairs, 8, QUERY_WIDTH), jnp.bfloat16),
        grid_spec=pltpu.PrefetchScalarGridSpec(
            num_scalar_prefetch=2,
            grid=(pairs,),
            in_specs=[
                pl.BlockSpec((64, 1, 8, 640), lambda i, *_: (0, i, 0, 0)),
                table,
                table,
                cache,
                cache,
            ],
            out_specs=pl.BlockSpec((1, 8, QUERY_WIDTH), lambda i, *_: (i, 0, 0)),
        ),
        compiler_params=pltpu.CompilerParams(vmem_limit_bytes=40 * 1024 * 1024),
        cost_estimate=pl.CostEstimate(
            flops=pairs * 8 * 8 * 64 * 512 * 128,
            bytes_accessed=pairs * 4 * 1024 * 1024,
            transcendentals=pairs * 8 * 64 * 512,
        ),
        name="attention",
    )(lengths, places, fields, cosine, sine, keys, values)


def block_places():
    z_index = lax.axis_index("zh") * 2 + lax.axis_index("zl")
    natural = jnp.arange(32, dtype=jnp.int32)
    zl, c, y, zh = natural >> 4, (natural >> 3) & 1, (natural >> 1) & 3, natural & 1
    plane = (zh * 2 + zl - z_index + 4) & 3
    core = (c - lax.axis_index("c") + 2) & 1
    return (plane * 2 + core) * 4 + y


def features_by_plane(rows):
    lead = rows.shape[:-1]
    nd = len(lead)
    z_index = lax.axis_index("zh") * 2 + lax.axis_index("zl")
    blocks = rows.reshape(*lead, 2, 2, 4, 2, 256)
    blocks = blocks.transpose(*range(nd), nd + 3, nd, nd + 1, nd + 2, nd + 4)
    blocks = blocks.reshape(*lead, Z_SIZE, 2, 1024)
    blocks = jnp.concatenate([blocks, blocks], axis=nd)
    blocks = lax.dynamic_slice_in_dim(blocks, z_index, Z_SIZE, axis=nd)
    return jnp.where(lax.axis_index("c") == 0, blocks, jnp.flip(blocks, axis=nd + 1))


def swap_cores(value):
    return lax.ppermute(value, "c", [(0, 1), (1, 0)])


def spread_depth(blocks):
    z_index = lax.axis_index("zh") * 2 + lax.axis_index("zl")
    zeros = (0,) * (blocks[0].ndim)
    rows = jnp.zeros((Z_SIZE,) + blocks[0].shape, blocks[0].dtype)
    rows = place(rows, blocks[0][None], z_index, *zeros)
    for step in (1, 2, 3):
        moved = shift_z(blocks[step], step)
        rows = place(rows, moved[None], (z_index - step + 4) & 3, *zeros)
    return rows


def body(
    hidden_states,
    norm_gain,
    lengths,
    rotated_key_cache,
    value_cache,
    qkv_weight,
    qkv_grad,
    qkv_first,
    qkv_second,
    out_weight,
    out_grad,
    out_first,
    out_second,
):
    depth = qkv_weight.shape[0]
    PLANE = ("y", "x")

    normed = features_by_plane(rms_norm(hidden_states, norm_gain))
    normed = normed.transpose(2, 1, 0, 3, 4).reshape(Z_SIZE, PAIRS, 8, 2048)

    qkv_updated = adam_step(qkv_weight, qkv_grad, qkv_first, qkv_second)
    qkv_piece = jnp.concatenate(
        [
            qkv_updated[:, :QUERY_WIDTH].reshape(depth, 16, 512),
            qkv_updated[:, QUERY_WIDTH:].reshape(depth, 16, 128),
        ],
        axis=2,
    ).transpose(1, 0, 2)
    qkv_own = lax.all_to_all(qkv_piece, PLANE, split_axis=0, concat_axis=0, tiled=True)
    qkv_own = qkv_own.reshape(16 * depth, 640)
    qkv_other = swap_cores(qkv_own)

    out_updated = adam_step(out_weight, out_grad, out_first, out_second)
    out_piece = out_updated.reshape(depth, 4, 2, 4, 256).transpose(1, 3, 0, 2, 4)
    out_piece = out_piece.reshape(16, depth, 512)
    out_own = lax.all_to_all(out_piece, PLANE, split_axis=0, concat_axis=0, tiled=True)
    out_own = out_own.reshape(16 * depth, 512)
    half = out_own.shape[0] // 2
    below = shift_z(out_own, 1)
    above = shift_z(out_own, -1)
    far = jnp.concatenate([shift_z(below[:half], 1), shift_z(above[half:], -1)], axis=0)
    out_planes = jnp.stack([out_own, above, far, below])
    out_owned = jnp.stack([out_planes, swap_cores(out_planes)], axis=1).reshape(D, 512)

    cosine, sine = rotary_tables(lengths)
    places = block_places()
    zh_index = lax.axis_index("zh")
    results = []
    for start, stop in CHUNKS:
        pairs = stop - start
        rows = spread_depth([normed[z, start:stop] for z in range(Z_SIZE)])
        rows = gather_plane(rows.reshape(Z_SIZE * pairs * 8, 2048))
        partial = jnp.dot(rows[:, :1024], qkv_own, preferred_element_type=jnp.float32) + jnp.dot(
            rows[:, 1024:], qkv_other, preferred_element_type=jnp.float32
        )
        partial = partial.astype(jnp.bfloat16).reshape(4, 4, 2, 2, pairs, 8, 640)
        partial = partial.transpose(3, 0, 2, 1, 4, 5, 6).reshape(64, pairs, 8, 640)
        fields = lax.all_to_all(
            partial, ("zl", "y", "zh", "x"), split_axis=0, concat_axis=0, tiled=True
        )
        attended = attention(
            fields, cosine, sine, rotated_key_cache, value_cache, lengths, places, start
        )
        rows = gather_plane(attended.reshape(pairs * 8, D))
        result = jnp.dot(rows, out_owned, preferred_element_type=jnp.float32)
        result = result.astype(jnp.bfloat16).reshape(4, 4, pairs, 2, DECODE_STEPS, 512)
        low, high = result[..., :256], result[..., 256:]
        kept = jnp.where(zh_index == 0, low, high)
        sent = jnp.where(zh_index == 0, high, low)
        came = lax.ppermute(sent, "zh", [(0, 1), (1, 0)])
        joined = jnp.stack(
            [jnp.where(zh_index == 0, kept, came), jnp.where(zh_index == 0, came, kept)], axis=1
        )
        results.append(joined)
    whole = jnp.concatenate(results, axis=3) if len(results) > 1 else results[0]
    return whole.transpose(5, 0, 1, 2, 3, 4, 6).reshape(DECODE_STEPS, -1, 256)


def solution(mesh):
    every = ("zl", "c", "y", "zh", "x")
    fine = jax.sharding.Mesh(mesh.devices.reshape(2, 2, 4, 2, 4), every)
    return jax.shard_map(
        body,
        mesh=fine,
        in_specs=(
            P(None, every, None),
            P(),
            P(every),
            P(every, None, None),
            P(every, None, None),
        )
        + (P(every, None),) * 8,
        out_specs=P(None, ("zl", "c"), ("y", "zh", "x")),
        check_vma=False,
    )
```

```python
import functools
import math

import jax
import jax.numpy as jnp
from jax import lax
from jax.experimental import pallas as pl
from jax.experimental.pallas import tpu as pltpu
from jax.sharding import PartitionSpec as P

D = 8192
HQ = 64
KEY_HEADS = 8
HEAD_SIZE = 128
CONTEXT_SLOTS = 512
DECODE_STEPS = 4
QUERY_WIDTH = 8192
KEY_WIDTH = 1024


learn_rate = 0.008
beta_one = 0.9
beta_two = 0.95
bias_one = 1.0 - beta_one * beta_one
bias_two = 1.0 - beta_two * beta_two
adam_eps = 1e-08
decay_rate = 0.1
rope_base = 500000.0
norm_eps = 1e-05


def adam_step(weight, gradient, moment_one, moment_two):
    grad_wide = gradient.astype(jnp.float32)
    first_new = beta_one * moment_one.astype(jnp.float32) + (1.0 - beta_one) * grad_wide
    second_new = (
        beta_two * moment_two.astype(jnp.float32) + (1.0 - beta_two) * grad_wide * grad_wide
    )
    weight_wide = weight.astype(jnp.float32)
    update = (
        first_new / bias_one / (jnp.sqrt(second_new / bias_two) + adam_eps)
        + decay_rate * weight_wide
    )
    return (weight_wide - learn_rate * update).astype(jnp.bfloat16)


PAIRS = 3
Z_SIZE = 4
PLANE = ("y", "x")


def shift_z(value, step):
    def position(z):
        return (z % 2) * 2 + (z // 2) % 2

    return lax.ppermute(
        value, ("zl", "zh"), [(position(z), position(z + step + Z_SIZE)) for z in range(Z_SIZE)]
    )


def swap_cores(value):
    return lax.ppermute(value, "c", [(0, 1), (1, 0)])


def norm_kernel(place_ref, hidden_ref, gain_ref, out_ref, scratch_ref):
    gain = gain_ref[...].astype(jnp.float32)
    rows = hidden_ref.shape[1]
    for step in range(DECODE_STEPS):
        wide = hidden_ref[step].astype(jnp.float32)
        inverse = lax.rsqrt(jnp.mean(wide * wide, axis=-1, keepdims=True) + norm_eps)
        normed = wide * inverse * gain
        for row in range(rows):
            at = row * DECODE_STEPS + step
            scratch_ref[at : at + 1, :] = normed[row : row + 1]
    for block in range(D // 256):
        start = pl.multiple_of(place_ref[block] * 256, 256)
        out_ref[:, pl.ds(start, 256)] = scratch_ref[
            :, block * 256 : (block + 1) * 256
        ].astype(jnp.bfloat16)


def norm_rows(hidden_states, norm_gain, places):
    rows = DECODE_STEPS * hidden_states.shape[1]
    vmem = pl.BlockSpec(memory_space=pltpu.VMEM)
    return pl.pallas_call(
        norm_kernel,
        out_shape=jax.ShapeDtypeStruct((rows, D), jnp.bfloat16),
        in_specs=[pl.BlockSpec(memory_space=pltpu.SMEM), vmem, vmem],
        out_specs=vmem,
        scratch_shapes=[pltpu.VMEM((rows, D), jnp.float32)],
        compiler_params=pltpu.CompilerParams(vmem_limit_bytes=16 * 1024 * 1024),
        name="norm_rows",
    )(places, hidden_states, norm_gain[None])


def rotary_tables(lengths):
    half_width = HEAD_SIZE // 2
    frequency = jnp.power(
        rope_base, -2.0 * jnp.arange(half_width, dtype=jnp.float32) / HEAD_SIZE
    )
    positions = lengths[:, None] + jnp.arange(DECODE_STEPS, dtype=jnp.int32)[None, :]
    angles = positions.astype(jnp.float32)[..., None] * frequency
    cosine, sine = jnp.cos(angles), jnp.sin(angles)
    shape = (PAIRS, 8, HEAD_SIZE)
    return (
        jnp.concatenate([cosine, cosine], axis=-1).reshape(shape),
        jnp.concatenate([-sine, sine], axis=-1).reshape(shape),
    )


def attention_kernel(lengths_ref, field_ref, cos_ref, sin_ref, key_ref, value_ref, out_ref):
    pair = pl.program_id(0)
    cosine, sine = cos_ref[0], sin_ref[0]
    scale = 1.0 / math.sqrt(HEAD_SIZE)
    row = lax.broadcasted_iota(jnp.int32, (64, 1), 0)
    second_row = ((row >> 2) & 1) == 1
    step = row & 3
    length = jnp.where(second_row, lengths_ref[2 * pair + 1], lengths_ref[2 * pair])
    live = lax.broadcasted_iota(jnp.int32, (64, CONTEXT_SLOTS), 1) < length
    fresh_column = lax.broadcasted_iota(jnp.int32, (64, 8), 1)
    fresh_live = (((fresh_column >> 2) & 1) == ((row >> 2) & 1)) & ((fresh_column & 3) <= step)

    def field(block, start):
        return field_ref[block, 0, :, start : start + 128].astype(jnp.float32)

    def rotate(vector):
        return vector * cosine + pltpu.roll(vector, 64, 1) * sine

    def times_transposed(left, right):
        return lax.dot_general(
            left, right, (((1,), (1,)), ((), ())), preferred_element_type=jnp.float32
        )

    for kv in range(KEY_HEADS):
        columns = slice(kv * HEAD_SIZE, (kv + 1) * HEAD_SIZE)
        query = jnp.concatenate(
            [rotate(field(2 * kv + h // 4, (h % 4) * 128)) for h in range(8)], axis=0
        ).astype(jnp.bfloat16)
        fresh_key = rotate(field(kv, 512)).astype(jnp.bfloat16)
        fresh_value = field(8 + kv, 512).astype(jnp.bfloat16)
        scores = jnp.where(
            second_row,
            times_transposed(query, key_ref[1, :, columns]),
            times_transposed(query, key_ref[0, :, columns]),
        ) * scale
        fresh_scores = times_transposed(query, fresh_key) * scale
        scores = jnp.where(live, scores, -jnp.inf)
        fresh_scores = jnp.where(fresh_live, fresh_scores, -jnp.inf)
        highest = jnp.maximum(
            jnp.max(scores, axis=-1, keepdims=True), jnp.max(fresh_scores, axis=-1, keepdims=True)
        )
        weight = jnp.exp(scores - highest)
        fresh_weight = jnp.exp(fresh_scores - highest)
        inverse = 1.0 / (
            jnp.sum(weight, axis=-1, keepdims=True) + jnp.sum(fresh_weight, axis=-1, keepdims=True)
        )
        prob = weight * inverse
        fresh_prob = (fresh_weight * inverse).astype(jnp.bfloat16)
        attended = (
            jnp.dot(
                jnp.where(second_row, 0.0, prob).astype(jnp.bfloat16),
                value_ref[0, :, columns],
                preferred_element_type=jnp.float32,
            )
            + jnp.dot(
                jnp.where(second_row, prob, 0.0).astype(jnp.bfloat16),
                value_ref[1, :, columns],
                preferred_element_type=jnp.float32,
            )
            + jnp.dot(fresh_prob, fresh_value, preferred_element_type=jnp.float32)
        )
        for h in range(0, 8, 2):
            natural = 4 * kv + h // 2
            y = (natural >> 1) & 3
            start = ((natural >> 3) * 2 + (natural & 1)) * 256
            block = jnp.concatenate(
                [attended[8 * h : 8 * h + 8], attended[8 * h + 8 : 8 * h + 16]], axis=1
            ).astype(jnp.bfloat16)
            for x in range(4):
                out_ref[4 * y + x, 0, :, start : start + 256] = block


def attention(fields, cosine, sine, keys, values, lengths):
    table = pl.BlockSpec((1, 8, HEAD_SIZE), lambda i, *_: (i, 0, 0))
    cache = pl.BlockSpec((2, CONTEXT_SLOTS, KEY_WIDTH), lambda i, *_: (i, 0, 0))
    return pl.pallas_call(
        attention_kernel,
        out_shape=jax.ShapeDtypeStruct((16, PAIRS, 8, 2048), jnp.bfloat16),
        grid_spec=pltpu.PrefetchScalarGridSpec(
            num_scalar_prefetch=1,
            grid=(PAIRS,),
            in_specs=[
                pl.BlockSpec((16, 1, 8, 640), lambda i, *_: (0, i, 0, 0)),
                table,
                table,
                cache,
                cache,
            ],
            out_specs=pl.BlockSpec((16, 1, 8, 2048), lambda i, *_: (0, i, 0, 0)),
        ),
        compiler_params=pltpu.CompilerParams(vmem_limit_bytes=40 * 1024 * 1024),
        cost_estimate=pl.CostEstimate(
            flops=PAIRS * 8 * 8 * 64 * 512 * 128,
            bytes_accessed=PAIRS * 4 * 1024 * 1024,
            transcendentals=PAIRS * 8 * 64 * 512,
        ),
        name="attention",
    )(lengths, fields, cosine, sine, keys, values)


def out_kernel(rows_ref, weight_ref, out_ref):
    out_ref[0] = jnp.dot(
        rows_ref[...], weight_ref[...], preferred_element_type=jnp.float32
    ).astype(jnp.bfloat16)


def out_partial(rows, weight):
    count, depth = rows.shape
    blocks = weight.shape[1] // 256
    return pl.pallas_call(
        out_kernel,
        out_shape=jax.ShapeDtypeStruct((blocks, count, 256), jnp.bfloat16),
        grid=(blocks,),
        in_specs=[
            pl.BlockSpec((count, depth), lambda i: (0, 0)),
            pl.BlockSpec((depth, 256), lambda i: (0, i)),
        ],
        out_specs=pl.BlockSpec((1, count, 256), lambda i: (i, 0, 0)),
        compiler_params=pltpu.CompilerParams(vmem_limit_bytes=24 * 1024 * 1024),
        cost_estimate=pl.CostEstimate(
            flops=2 * count * depth * blocks * 256,
            bytes_accessed=2 * depth * blocks * 256,
            transcendentals=0,
        ),
        name="out_partial",
    )(rows, weight)


def block_places():
    z_index = lax.axis_index("zh") * 2 + lax.axis_index("zl")
    natural = jnp.arange(32, dtype=jnp.int32)
    zl, c, y, zh = natural >> 4, (natural >> 3) & 1, (natural >> 1) & 3, natural & 1
    plane = (zh * 2 + zl - z_index + 4) & 3
    core = (c - lax.axis_index("c") + 2) & 1
    return (plane * 2 + core) * 4 + y


def body(
    hidden_states,
    norm_gain,
    lengths,
    rotated_key_cache,
    value_cache,
    qkv_weight,
    qkv_grad,
    qkv_first,
    qkv_second,
    out_weight,
    out_grad,
    out_first,
    out_second,
):
    depth = qkv_weight.shape[0]

    normed = norm_rows(hidden_states, norm_gain, block_places())
    normed_rows = lax.all_gather(normed, PLANE, axis=0, tiled=True)

    qkv_updated = adam_step(qkv_weight, qkv_grad, qkv_first, qkv_second)
    qkv_piece = jnp.concatenate(
        [
            qkv_updated[:, :QUERY_WIDTH].reshape(depth, 16, 512),
            qkv_updated[:, QUERY_WIDTH:].reshape(depth, 16, 128),
        ],
        axis=2,
    ).transpose(1, 0, 2)
    qkv_own = lax.all_to_all(qkv_piece, PLANE, split_axis=0, concat_axis=0, tiled=True)
    qkv_own = qkv_own.reshape(16 * depth, 640)
    half = qkv_own.shape[0] // 2
    below = shift_z(qkv_own, 1)
    above = shift_z(qkv_own, -1)

    out_updated = adam_step(out_weight, out_grad, out_first, out_second)
    out_piece = out_updated.reshape(depth, 8, 4, 256).transpose(2, 0, 1, 3).reshape(4, depth, 2048)
    out_piece, qkv_own = lax.optimization_barrier((out_piece, qkv_own))
    out_own = lax.all_to_all(out_piece, "x", split_axis=0, concat_axis=0, tiled=True)
    out_own = out_own.reshape(4 * depth, 2048)

    far = jnp.concatenate([shift_z(below[:half], 1), shift_z(above[half:], -1)], axis=0)
    cosine, sine = rotary_tables(lengths)
    far, out_own, cosine, sine = lax.optimization_barrier((far, out_own, cosine, sine))
    out_owned = lax.all_gather(out_own, ("zl", "c", "zh"), axis=0, tiled=True)

    projected = None
    for plane, weight in ((0, qkv_own), (1, above), (3, below), (2, far)):
        for core, part in enumerate((weight, swap_cores(weight))):
            start = (2 * plane + core) * 1024
            term = jnp.dot(
                normed_rows[:, start : start + 1024], part, preferred_element_type=jnp.float32
            )
            projected = term if projected is None else projected + term
    projected = projected.astype(jnp.bfloat16).reshape(16, -1, 640)
    fields = lax.all_to_all(projected, PLANE, split_axis=0, concat_axis=0, tiled=True)

    attended = attention(
        fields.reshape(16, PAIRS, 8, 640), cosine, sine, rotated_key_cache, value_cache, lengths
    )
    attended = lax.all_to_all(attended, PLANE, split_axis=0, concat_axis=0, tiled=True)
    partial = out_partial(attended.reshape(-1, 2048), out_owned)
    partial = lax.all_to_all(partial, ("y", "zh"), split_axis=0, concat_axis=0, tiled=True)
    total = jnp.sum(partial.reshape(4, 2, -1, 256).astype(jnp.float32), axis=0)
    total = total.astype(jnp.bfloat16).reshape(2, 4, 4, -1, DECODE_STEPS, 256)
    return total.transpose(4, 1, 0, 2, 3, 5).reshape(DECODE_STEPS, -1, 256)


def solution(mesh):
    every = ("zl", "c", "y", "zh", "x")
    fine = jax.sharding.Mesh(mesh.devices.reshape(2, 2, 4, 2, 4), every)
    return jax.shard_map(
        body,
        mesh=fine,
        in_specs=(
            P(None, every, None),
            P(),
            P(every),
            P(every, None, None),
            P(every, None, None),
        )
        + (P(every, None),) * 8,
        out_specs=P(None, ("zl", "c"), ("y", "zh", "x")),
        check_vma=False,
    )
```

```python
import functools
import math

import jax
import jax.numpy as jnp
from jax import lax
from jax.experimental import pallas as pl
from jax.experimental.pallas import tpu as pltpu
from jax.sharding import PartitionSpec as P

D = 8192
HQ = 64
KEY_HEADS = 8
HEAD_SIZE = 128
CONTEXT_SLOTS = 512
DECODE_STEPS = 4
QUERY_WIDTH = 8192
KEY_WIDTH = 1024


learn_rate = 0.008
beta_one = 0.9
beta_two = 0.95
bias_one = 1.0 - beta_one * beta_one
bias_two = 1.0 - beta_two * beta_two
adam_eps = 1e-08
decay_rate = 0.1
rope_base = 500000.0
norm_eps = 1e-05


def adam_step(weight, gradient, moment_one, moment_two):
    grad_wide = gradient.astype(jnp.float32)
    first_new = beta_one * moment_one.astype(jnp.float32) + (1.0 - beta_one) * grad_wide
    second_new = (
        beta_two * moment_two.astype(jnp.float32) + (1.0 - beta_two) * grad_wide * grad_wide
    )
    weight_wide = weight.astype(jnp.float32)
    update = (
        first_new / bias_one / (jnp.sqrt(second_new / bias_two) + adam_eps)
        + decay_rate * weight_wide
    )
    return (weight_wide - learn_rate * update).astype(jnp.bfloat16)


PAIRS = 3
Z_SIZE = 4
PLANE = ("y", "x")
VMEM_LIMIT = 56 * 1024 * 1024


def shift_z(value, step):
    def position(z):
        return (z % 2) * 2 + (z // 2) % 2

    return lax.ppermute(
        value, ("zl", "zh"), [(position(z), position(z + step + Z_SIZE)) for z in range(Z_SIZE)]
    )


def swap_cores(value):
    return lax.ppermute(value, "c", [(0, 1), (1, 0)])


def norm_kernel(place_ref, hidden_ref, gain_ref, out_ref, scratch_ref):
    gain = gain_ref[...].astype(jnp.float32)
    rows = hidden_ref.shape[1]
    for step in range(DECODE_STEPS):
        wide = hidden_ref[step].astype(jnp.float32)
        inverse = lax.rsqrt(jnp.mean(wide * wide, axis=-1, keepdims=True) + norm_eps)
        normed = wide * inverse * gain
        for row in range(rows):
            at = row * DECODE_STEPS + step
            scratch_ref[at : at + 1, :] = normed[row : row + 1]
    for natural in range(D // 256):
        start = pl.multiple_of(place_ref[natural] * 256, 256)
        block = scratch_ref[:, natural * 256 : (natural + 1) * 256].astype(jnp.bfloat16)
        for x in range(4):
            out_ref[4 * ((natural >> 1) & 3) + x, :, pl.ds(start, 256)] = block


def norm_rows(hidden_states, norm_gain, places):
    rows = DECODE_STEPS * hidden_states.shape[1]
    vmem = pl.BlockSpec(memory_space=pltpu.VMEM)
    return pl.pallas_call(
        norm_kernel,
        out_shape=jax.ShapeDtypeStruct((16, rows, D // 4), jnp.bfloat16),
        in_specs=[pl.BlockSpec(memory_space=pltpu.SMEM), vmem, vmem],
        out_specs=vmem,
        scratch_shapes=[pltpu.VMEM((rows, D), jnp.float32)],
        compiler_params=pltpu.CompilerParams(vmem_limit_bytes=16 * 1024 * 1024),
        name="norm_rows",
    )(places, hidden_states, norm_gain[None])


def rotary_tables(lengths):
    half_width = HEAD_SIZE // 2
    frequency = jnp.power(
        rope_base, -2.0 * jnp.arange(half_width, dtype=jnp.float32) / HEAD_SIZE
    )
    positions = lengths[:, None] + jnp.arange(DECODE_STEPS, dtype=jnp.int32)[None, :]
    angles = positions.astype(jnp.float32)[..., None] * frequency
    cosine, sine = jnp.cos(angles), jnp.sin(angles)
    shape = (PAIRS, 8, HEAD_SIZE)
    return (
        jnp.concatenate([cosine, cosine], axis=-1).reshape(shape),
        jnp.concatenate([-sine, sine], axis=-1).reshape(shape),
    )


def attention_kernel(
    lengths_ref, place_ref, field_ref, cos_ref, sin_ref, key_ref, value_ref, out_ref
):
    pair = pl.program_id(0)
    cosine, sine = cos_ref[0], sin_ref[0]
    scale = 1.0 / math.sqrt(HEAD_SIZE)
    line = lax.broadcasted_iota(jnp.int32, (128, 1), 0)
    second_row = ((line >> 2) & 1) == 1
    step = line & 3
    length = jnp.where(second_row, lengths_ref[2 * pair + 1], lengths_ref[2 * pair])
    live = lax.broadcasted_iota(jnp.int32, (128, CONTEXT_SLOTS), 1) < length
    fresh_column = lax.broadcasted_iota(jnp.int32, (128, 8), 1)
    fresh_live = (((fresh_column >> 2) & 1) == ((line >> 2) & 1)) & ((fresh_column & 3) <= step)

    def field(x, start):
        total = None
        for y in range(4):
            term = field_ref[4 * y + x, 0, :, start : start + 128].astype(jnp.float32)
            total = term if total is None else total + term
        return total.astype(jnp.bfloat16).astype(jnp.float32)

    def rotate(vector):
        return vector * cosine + pltpu.roll(vector, 64, 1) * sine

    def times_transposed(left, right):
        return lax.dot_general(
            left, right, (((1,), (1,)), ((), ())), preferred_element_type=jnp.float32
        )

    for x in range(KEY_HEADS // 2):
        cached, fresh, fresh_values = [], [], []
        for side in range(2):
            kv = 2 * x + side
            columns = slice(kv * HEAD_SIZE, (kv + 1) * HEAD_SIZE)
            query = jnp.concatenate(
                [rotate(field(x, (8 * side + h) * 128)) for h in range(8)], axis=0
            ).astype(jnp.bfloat16)
            fresh_key = rotate(field(x, 2048 + 128 * side)).astype(jnp.bfloat16)
            fresh_values.append(field(x, 2304 + 128 * side))
            cached.append(
                jnp.where(
                    second_row[:64],
                    times_transposed(query, key_ref[1, :, columns]),
                    times_transposed(query, key_ref[0, :, columns]),
                )
            )
            fresh.append(times_transposed(query, fresh_key))
        scores = jnp.where(live, jnp.concatenate(cached, axis=0) * scale, -jnp.inf)
        fresh_scores = jnp.where(fresh_live, jnp.concatenate(fresh, axis=0) * scale, -jnp.inf)
        highest = jnp.maximum(
            jnp.max(scores, axis=-1, keepdims=True), jnp.max(fresh_scores, axis=-1, keepdims=True)
        )
        weight = jnp.exp(scores - highest)
        fresh_weight = jnp.exp(fresh_scores - highest)
        inverse = 1.0 / (
            jnp.sum(weight, axis=-1, keepdims=True) + jnp.sum(fresh_weight, axis=-1, keepdims=True)
        )
        prob = weight * inverse
        fresh_prob = (fresh_weight * inverse).astype(jnp.bfloat16)
        columns = slice(x * 256, (x + 1) * 256)
        attended = (
            jnp.dot(
                jnp.where(second_row, 0.0, prob).astype(jnp.bfloat16),
                value_ref[0, :, columns],
                preferred_element_type=jnp.float32,
            )
            + jnp.dot(
                jnp.where(second_row, prob, 0.0).astype(jnp.bfloat16),
                value_ref[1, :, columns],
                preferred_element_type=jnp.float32,
            )
            + jnp.dot(
                fresh_prob,
                jnp.concatenate(fresh_values, axis=1).astype(jnp.bfloat16),
                preferred_element_type=jnp.float32,
            )
        )
        for h in range(0, 16, 2):
            natural = 8 * x + h // 2
            y = (natural >> 1) & 3
            start = pl.multiple_of(place_ref[natural] * 256, 256)
            side = slice(128 * (h // 8), 128 * (h // 8) + 128)
            block = jnp.concatenate(
                [attended[8 * h : 8 * h + 8, side], attended[8 * h + 8 : 8 * h + 16, side]], axis=1
            ).astype(jnp.bfloat16)
            for copy in range(4):
                out_ref[4 * y + copy, 0, :, pl.ds(start, 256)] = block


def attention(fields, cosine, sine, keys, values, lengths, places):
    table = pl.BlockSpec((1, 8, HEAD_SIZE), lambda i, *_: (i, 0, 0))
    cache = pl.BlockSpec((2, CONTEXT_SLOTS, KEY_WIDTH), lambda i, *_: (i, 0, 0))
    return pl.pallas_call(
        attention_kernel,
        out_shape=jax.ShapeDtypeStruct((16, PAIRS, 8, 2048), jnp.bfloat16),
        grid_spec=pltpu.PrefetchScalarGridSpec(
            num_scalar_prefetch=2,
            grid=(PAIRS,),
            in_specs=[
                pl.BlockSpec((16, 1, 8, 2560), lambda i, *_: (0, i, 0, 0)),
                table,
                table,
                cache,
                cache,
            ],
            out_specs=pl.BlockSpec((16, 1, 8, 2048), lambda i, *_: (0, i, 0, 0)),
        ),
        compiler_params=pltpu.CompilerParams(vmem_limit_bytes=VMEM_LIMIT),
        cost_estimate=pl.CostEstimate(
            flops=PAIRS * 8 * 8 * 64 * 512 * 128,
            bytes_accessed=PAIRS * 4 * 1024 * 1024,
            transcendentals=PAIRS * 8 * 64 * 512,
        ),
        name="attention",
    )(lengths, places, fields, cosine, sine, keys, values)


def product_kernel(starts, rows_ref, *refs):
    pieces, out_ref = refs[:-1], refs[-1]
    total = None
    for start, piece in zip(starts, pieces):
        term = jnp.dot(
            rows_ref[:, start : start + piece.shape[0]],
            piece[...],
            preferred_element_type=jnp.float32,
        )
        total = term if total is None else total + term
    out_ref[...] = total.astype(jnp.bfloat16).reshape(out_ref.shape)


def product(rows, pieces, by_block, name):
    starts = tuple(start for start, _ in pieces)
    weights = [weight for _, weight in pieces]
    count, depth = rows.shape
    columns = weights[0].shape[1]
    blocks = columns // 256
    if by_block:
        out_shape, out_spec = (blocks, count, 256), pl.BlockSpec((1, count, 256), lambda i: (i, 0, 0))
    else:
        out_shape, out_spec = (count, columns), pl.BlockSpec((count, 256), lambda i: (0, i))
    return pl.pallas_call(
        functools.partial(product_kernel, starts),
        out_shape=jax.ShapeDtypeStruct(out_shape, jnp.bfloat16),
        grid=(blocks,),
        in_specs=[pl.BlockSpec((count, depth), lambda i: (0, 0))]
        + [pl.BlockSpec((weight.shape[0], 256), lambda i: (0, i)) for weight in weights],
        out_specs=out_spec,
        compiler_params=pltpu.CompilerParams(vmem_limit_bytes=VMEM_LIMIT),
        cost_estimate=pl.CostEstimate(
            flops=2 * count * depth * columns,
            bytes_accessed=2 * depth * (count + columns),
            transcendentals=0,
        ),
        name=name,
    )(rows, *weights)


def depth_pieces(own, above, below, far):
    depth = own.shape[0]
    half = far[0].shape[0]
    pieces = []
    for start, weight in (
        (0, own),
        (2 * depth, above),
        (6 * depth, below),
        (4 * depth, far[0]),
        (4 * depth + half, far[1]),
    ):
        pieces += [(start, weight), (start + depth, swap_cores(weight))]
    return pieces


def block_places():
    z_index = lax.axis_index("zh") * 2 + lax.axis_index("zl")
    natural = jnp.arange(32, dtype=jnp.int32)
    zl, c, y, zh = natural >> 4, (natural >> 3) & 1, (natural >> 1) & 3, natural & 1
    plane = (zh * 2 + zl - z_index + 4) & 3
    core = (c - lax.axis_index("c") + 2) & 1
    return (plane * 2 + core) * 4 + y


def body(
    hidden_states,
    norm_gain,
    lengths,
    rotated_key_cache,
    value_cache,
    qkv_weight,
    qkv_grad,
    qkv_first,
    qkv_second,
    out_weight,
    out_grad,
    out_first,
    out_second,
):
    depth = qkv_weight.shape[0]

    places = block_places() >> 2
    qkv_updated = adam_step(qkv_weight, qkv_grad, qkv_first, qkv_second)
    qkv_piece = jnp.concatenate(
        [
            qkv_updated[:, :QUERY_WIDTH].reshape(depth, 4, 2048),
            qkv_updated[:, QUERY_WIDTH : QUERY_WIDTH + KEY_WIDTH].reshape(depth, 4, 256),
            qkv_updated[:, QUERY_WIDTH + KEY_WIDTH :].reshape(depth, 4, 256),
        ],
        axis=2,
    ).transpose(1, 0, 2)
    qkv_own = lax.all_to_all(qkv_piece, "x", split_axis=0, concat_axis=0, tiled=True)
    qkv_own = qkv_own.reshape(4 * depth, 2560)
    normed = norm_rows(hidden_states, norm_gain, places)
    out_updated = adam_step(out_weight, out_grad, out_first, out_second)
    out_piece = out_updated.reshape(depth, 8, 4, 256).transpose(2, 0, 1, 3).reshape(4, depth, 2048)
    qkv_own, normed, out_piece = lax.optimization_barrier((qkv_own, normed, out_piece))

    half = qkv_own.shape[0] // 2
    below = shift_z(qkv_own, 1)
    above = shift_z(qkv_own, -1)
    normed_rows = lax.all_to_all(normed, PLANE, split_axis=0, concat_axis=0, tiled=True)
    below, above, normed_rows = lax.optimization_barrier((below, above, normed_rows))
    far = shift_z(below[:half], 1), shift_z(above[half:], -1)
    out_piece, _ = lax.optimization_barrier((out_piece, normed_rows))
    out_own = lax.all_to_all(out_piece, "x", split_axis=0, concat_axis=0, tiled=True)
    out_own = out_own.reshape(4 * depth, 2048)
    cosine, sine = rotary_tables(lengths)
    far, out_own, cosine, sine = lax.optimization_barrier((far, out_own, cosine, sine))
    out_below = shift_z(out_own, 1)
    out_above = shift_z(out_own, -1)

    projected = product(
        normed_rows.reshape(-1, 2048), depth_pieces(qkv_own, above, below, far), False, "qkv_partial"
    )
    fields = lax.all_to_all(
        projected.reshape(16, -1, 2560), PLANE, split_axis=0, concat_axis=0, tiled=True
    )

    fields, out_below, out_above = lax.optimization_barrier((fields, out_below, out_above))
    out_far = shift_z(out_below[:half], 1), shift_z(out_above[half:], -1)
    attended = attention(
        fields.reshape(16, PAIRS, 8, 2560),
        cosine,
        sine,
        rotated_key_cache,
        value_cache,
        lengths,
        places,
    )
    attended, out_far = lax.optimization_barrier((attended, out_far))
    attended = lax.all_to_all(attended, PLANE, split_axis=0, concat_axis=0, tiled=True)
    partial = product(
        attended.reshape(-1, 2048),
        depth_pieces(out_own, out_above, out_below, out_far),
        True,
        "out_partial",
    )
    partial = lax.all_to_all(partial, ("y", "zh"), split_axis=0, concat_axis=0, tiled=True)
    total = jnp.sum(partial.reshape(4, 2, -1, 256).astype(jnp.float32), axis=0)
    total = total.astype(jnp.bfloat16).reshape(2, 4, 4, -1, DECODE_STEPS, 256)
    return total.transpose(4, 1, 0, 2, 3, 5).reshape(DECODE_STEPS, -1, 256)


def solution(mesh):
    every = ("zl", "c", "y", "zh", "x")
    fine = jax.sharding.Mesh(mesh.devices.reshape(2, 2, 4, 2, 4), every)
    return jax.shard_map(
        body,
        mesh=fine,
        in_specs=(
            P(None, every, None),
            P(),
            P(every),
            P(every, None, None),
            P(every, None, None),
        )
        + (P(every, None),) * 8,
        out_specs=P(None, ("zl", "c"), ("y", "zh", "x")),
        check_vma=False,
    )
```

```python
import functools
import math

import jax
import jax.numpy as jnp
from jax import lax
from jax.experimental import pallas as pl
from jax.experimental.pallas import tpu as pltpu
from jax.sharding import PartitionSpec as P

D = 8192
HQ = 64
KEY_HEADS = 8
HEAD_SIZE = 128
CONTEXT_SLOTS = 512
DECODE_STEPS = 4
QUERY_WIDTH = 8192
KEY_WIDTH = 1024


learn_rate = 0.008
beta_one = 0.9
beta_two = 0.95
bias_one = 1.0 - beta_one * beta_one
bias_two = 1.0 - beta_two * beta_two
adam_eps = 1e-08
decay_rate = 0.1
rope_base = 500000.0
norm_eps = 1e-05


def adam_step(weight, gradient, moment_one, moment_two):
    grad_wide = gradient.astype(jnp.float32)
    first_new = beta_one * moment_one.astype(jnp.float32) + (1.0 - beta_one) * grad_wide
    second_new = (
        beta_two * moment_two.astype(jnp.float32) + (1.0 - beta_two) * grad_wide * grad_wide
    )
    weight_wide = weight.astype(jnp.float32)
    update = (
        first_new / bias_one / (jnp.sqrt(second_new / bias_two) + adam_eps)
        + decay_rate * weight_wide
    )
    return (weight_wide - learn_rate * update).astype(jnp.bfloat16)


PAIRS = 3
Z_SIZE = 4
PLANE = ("y", "x")
VMEM_LIMIT = 56 * 1024 * 1024


def shift_z(value, step):
    def position(z):
        return (z % 2) * 2 + (z // 2) % 2

    return lax.ppermute(
        value, ("zl", "zh"), [(position(z), position(z + step + Z_SIZE)) for z in range(Z_SIZE)]
    )


def swap_cores(value):
    return lax.ppermute(value, "c", [(0, 1), (1, 0)])


def joint_adam_kernel(*refs):
    out_ref = refs[-1]
    query, key, value = (
        adam_step(*(ref[...] for ref in refs[part:12:3])) for part in range(3)
    )
    for x in range(2):
        out_ref[x, :, :1024] = query[:, x * 1024 : (x + 1) * 1024]
        out_ref[x, :, 1024:1152] = key[:, x * 128 : (x + 1) * 128]
        out_ref[x, :, 1152:] = value[:, x * 128 : (x + 1) * 128]


def joint_adam(half, *arrays):
    depth = arrays[0].shape[0]
    specs = [
        pl.BlockSpec((depth, 2048), lambda i: (0, 2 * half + i)),
        pl.BlockSpec((depth, 256), lambda i: (0, 32 + 2 * half + i)),
        pl.BlockSpec((depth, 256), lambda i: (0, 36 + 2 * half + i)),
    ]
    return pl.pallas_call(
        joint_adam_kernel,
        out_shape=jax.ShapeDtypeStruct((4, depth, 1280), jnp.bfloat16),
        grid=(2,),
        in_specs=specs * 4,
        out_specs=pl.BlockSpec((2, depth, 1280), lambda i: (i, 0, 0)),
        compiler_params=pltpu.CompilerParams(vmem_limit_bytes=VMEM_LIMIT),
        name="joint_adam",
    )(*(array for array in arrays for _ in range(3)))


def norm_kernel(hidden_ref, gain_ref, out_ref, scratch_ref):
    gain = gain_ref[...].astype(jnp.float32)
    rows = hidden_ref.shape[1]
    for step in range(DECODE_STEPS):
        wide = hidden_ref[step].astype(jnp.float32)
        inverse = lax.rsqrt(jnp.mean(wide * wide, axis=-1, keepdims=True) + norm_eps)
        normed = wide * inverse * gain
        for row in range(rows):
            at = row * DECODE_STEPS + step
            scratch_ref[at : at + 1, :] = normed[row : row + 1]
    for natural in range(D // 256):
        start = ((natural >> 3) * 2 + (natural & 1)) * 256
        block = scratch_ref[:, natural * 256 : (natural + 1) * 256].astype(jnp.bfloat16)
        for x in range(4):
            out_ref[4 * ((natural >> 1) & 3) + x, :, start : start + 256] = block


def norm_rows(hidden_states, norm_gain):
    rows = DECODE_STEPS * hidden_states.shape[1]
    vmem = pl.BlockSpec(memory_space=pltpu.VMEM)
    return pl.pallas_call(
        norm_kernel,
        out_shape=jax.ShapeDtypeStruct((16, rows, D // 4), jnp.bfloat16),
        in_specs=[vmem, vmem],
        out_specs=vmem,
        scratch_shapes=[pltpu.VMEM((rows, D), jnp.float32)],
        compiler_params=pltpu.CompilerParams(vmem_limit_bytes=16 * 1024 * 1024),
        name="norm_rows",
    )(hidden_states, norm_gain[None])


def rotary_tables(lengths):
    half_width = HEAD_SIZE // 2
    frequency = jnp.power(
        rope_base, -2.0 * jnp.arange(half_width, dtype=jnp.float32) / HEAD_SIZE
    )
    positions = lengths[:, None] + jnp.arange(DECODE_STEPS, dtype=jnp.int32)[None, :]
    angles = positions.astype(jnp.float32)[..., None] * frequency
    cosine, sine = jnp.cos(angles), jnp.sin(angles)
    shape = (PAIRS, 8, HEAD_SIZE)
    return (
        jnp.concatenate([cosine, cosine], axis=-1).reshape(shape),
        jnp.concatenate([-sine, sine], axis=-1).reshape(shape),
    )


def attention_kernel(
    lengths_ref, field_ref, cos_ref, sin_ref, key_ref, value_ref, *refs
):
    out_ref = refs[-1]
    pair = pl.program_id(0)
    cosine, sine = cos_ref[0], sin_ref[0]
    scale = 1.0 / math.sqrt(HEAD_SIZE)
    line = lax.broadcasted_iota(jnp.int32, (128, 1), 0)
    second_row = ((line >> 2) & 1) == 1
    step = line & 3
    length = jnp.where(second_row, lengths_ref[2 * pair + 1], lengths_ref[2 * pair])
    live = lax.broadcasted_iota(jnp.int32, (128, CONTEXT_SLOTS), 1) < length
    fresh_column = lax.broadcasted_iota(jnp.int32, (128, 8), 1)
    fresh_live = (((fresh_column >> 2) & 1) == ((line >> 2) & 1)) & ((fresh_column & 3) <= step)

    def field(x, start):
        total = None
        for y in range(4):
            term = field_ref[4 * y + x, 0, :, start : start + 128].astype(jnp.float32)
            total = term if total is None else total + term
        return total.astype(jnp.bfloat16).astype(jnp.float32)

    def rotate(vector):
        return vector * cosine + pltpu.roll(vector, 64, 1) * sine

    def times_transposed(left, right):
        return lax.dot_general(
            left, right, (((1,), (1,)), ((), ())), preferred_element_type=jnp.float32
        )

    for first in range(0, KEY_HEADS // 2, 2):
        cached, fresh, fresh_values = [], [], []
        for kv in (first, first + 1):
            columns = slice(kv * HEAD_SIZE, (kv + 1) * HEAD_SIZE)
            query = jnp.concatenate(
                [rotate(field(kv, h * 128)) for h in range(8)], axis=0
            ).astype(jnp.bfloat16)
            fresh_key = rotate(field(kv, 1024)).astype(jnp.bfloat16)
            fresh_values.append(field(kv, 1152))
            cached.append(
                jnp.where(
                    second_row[:64],
                    times_transposed(query, key_ref[1, :, columns]),
                    times_transposed(query, key_ref[0, :, columns]),
                )
            )
            fresh.append(times_transposed(query, fresh_key))
        scores = jnp.where(live, jnp.concatenate(cached, axis=0) * scale, -jnp.inf)
        fresh_scores = jnp.where(fresh_live, jnp.concatenate(fresh, axis=0) * scale, -jnp.inf)
        highest = jnp.maximum(
            jnp.max(scores, axis=-1, keepdims=True), jnp.max(fresh_scores, axis=-1, keepdims=True)
        )
        weight = jnp.exp(scores - highest)
        fresh_weight = jnp.exp(fresh_scores - highest)
        inverse = 1.0 / (
            jnp.sum(weight, axis=-1, keepdims=True) + jnp.sum(fresh_weight, axis=-1, keepdims=True)
        )
        prob = weight * inverse
        fresh_prob = (fresh_weight * inverse).astype(jnp.bfloat16)
        columns = slice(first * 128, first * 128 + 256)
        attended = (
            jnp.dot(
                jnp.where(second_row, 0.0, prob).astype(jnp.bfloat16),
                value_ref[0, :, columns],
                preferred_element_type=jnp.float32,
            )
            + jnp.dot(
                jnp.where(second_row, prob, 0.0).astype(jnp.bfloat16),
                value_ref[1, :, columns],
                preferred_element_type=jnp.float32,
            )
            + jnp.dot(
                fresh_prob,
                jnp.concatenate(fresh_values, axis=1).astype(jnp.bfloat16),
                preferred_element_type=jnp.float32,
            )
        )
        for h in range(0, 16, 2):
            natural = 4 * first + h // 2
            y = (natural >> 1) & 3
            start = ((natural >> 3) * 2 + (natural & 1)) * 256
            side = slice(128 * (h // 8), 128 * (h // 8) + 128)
            block = jnp.concatenate(
                [attended[8 * h : 8 * h + 8, side], attended[8 * h + 8 : 8 * h + 16, side]], axis=1
            ).astype(jnp.bfloat16)
            for copy in range(4):
                out_ref[4 * y + copy, 0, :, start : start + 256] = block


def attention(half, fields, cosine, sine, keys, values, lengths, *before):
    table = pl.BlockSpec((1, 8, HEAD_SIZE), lambda i, *_: (i, 0, 0))
    cache = pl.BlockSpec((2, CONTEXT_SLOTS, KEY_WIDTH // 2), lambda i, *_: (i, 0, half))
    return pl.pallas_call(
        attention_kernel,
        out_shape=jax.ShapeDtypeStruct((16, PAIRS, 8, 2048), jnp.bfloat16),
        grid_spec=pltpu.PrefetchScalarGridSpec(
            num_scalar_prefetch=1,
            grid=(PAIRS,),
            in_specs=[
                pl.BlockSpec((16, 1, 8, 1280), lambda i, *_: (0, i, 0, 0)),
                table,
                table,
                cache,
                cache,
            ]
            + [pl.BlockSpec(memory_space=pl.ANY)] * len(before),
            out_specs=pl.BlockSpec((16, 1, 8, 1024), lambda i, *_: (0, i, 0, half)),
        ),
        input_output_aliases={6: 0} if before else {},
        compiler_params=pltpu.CompilerParams(vmem_limit_bytes=VMEM_LIMIT),
        cost_estimate=pl.CostEstimate(
            flops=PAIRS * 4 * 8 * 64 * 512 * 128,
            bytes_accessed=PAIRS * 2 * 1024 * 1024,
            transcendentals=PAIRS * 4 * 64 * 512,
        ),
        name="attention",
    )(lengths, fields, cosine, sine, keys, values, *before)


def product_kernel(parts, places, by_block, start_ref, *refs):
    rows, pieces = refs[:parts], refs[parts : parts + len(places)]
    out_ref, rows_held, held, row_sems, piece_sems = refs[parts + len(places) :]
    width = rows[0].shape[1]
    row_copies = [
        pltpu.make_async_copy(part, rows_held.at[:, pl.ds(i * width, width)], row_sems.at[i])
        for i, part in enumerate(rows)
    ]
    for copy in row_copies:
        copy.start()

    blocks, columns = held.shape[0], held.shape[2]

    def copies(block):
        for i, (piece, (index, offset)) in enumerate(zip(pieces, places)):
            start = pl.multiple_of(start_ref[index] + offset, 128)
            yield pltpu.make_async_copy(
                piece.at[:, pl.ds(block * columns, columns)],
                held.at[block, pl.ds(start, piece.shape[0]), :],
                piece_sems.at[block, i],
            )

    for block in range(blocks):
        for copy in copies(block):
            copy.start()
    for copy in row_copies:
        copy.wait()
    for block in range(blocks):
        for copy in copies(block):
            copy.wait()
        for part in range(columns // 256):
            result = jnp.dot(
                rows_held[...],
                held[block, :, part * 256 : (part + 1) * 256],
                preferred_element_type=jnp.float32,
            ).astype(jnp.bfloat16)
            at = block * (columns // 256) + part
            if by_block:
                out_ref[at] = result
            else:
                out_ref[:, at * 256 : (at + 1) * 256] = result


def product(rows, pieces, starts, turns, by_block, name):
    places = tuple(place for place, _ in pieces)
    weights = [weight for _, weight in pieces]
    count, depth = rows[0].shape[0], sum(part.shape[1] for part in rows)
    columns = weights[0].shape[1]
    blocks = columns // 256
    anywhere = pl.BlockSpec(memory_space=pl.ANY)
    return pl.pallas_call(
        functools.partial(product_kernel, len(rows), places, by_block),
        out_shape=jax.ShapeDtypeStruct(
            (blocks, count, 256) if by_block else (count, columns), jnp.bfloat16
        ),
        in_specs=[pl.BlockSpec(memory_space=pltpu.SMEM)] + [anywhere] * (len(rows) + len(weights)),
        out_specs=pl.BlockSpec(memory_space=pltpu.VMEM),
        scratch_shapes=[
            pltpu.VMEM((count, depth), jnp.bfloat16),
            pltpu.VMEM((turns, depth, columns // turns), jnp.bfloat16),
            pltpu.SemaphoreType.DMA((len(rows),)),
            pltpu.SemaphoreType.DMA((turns, len(weights))),
        ],
        compiler_params=pltpu.CompilerParams(vmem_limit_bytes=VMEM_LIMIT),
        cost_estimate=pl.CostEstimate(
            flops=2 * count * depth * columns,
            bytes_accessed=2 * depth * (count + columns),
            transcendentals=0,
        ),
        name=name,
    )(starts, *rows, *weights)


def piece_starts(size):
    ahead = jnp.arange(8, dtype=jnp.int32)
    plane = (lax.axis_index("zh") * 2 + lax.axis_index("zl") + (ahead >> 1)) & 3
    core = (lax.axis_index("c") + ahead) & 1
    return ((plane & 1) * 4 + core * 2 + (plane >> 1)) * size


def both_cores(*pieces):
    result = []
    for plane, offset, own, other in pieces:
        result += [((2 * plane, offset), own), ((2 * plane + 1, offset), other)]
    return result


def body(
    hidden_states,
    norm_gain,
    lengths,
    rotated_key_cache,
    value_cache,
    qkv_weight,
    qkv_grad,
    qkv_first,
    qkv_second,
    out_weight,
    out_grad,
    out_first,
    out_second,
):
    depth = qkv_weight.shape[0]
    barrier = lax.optimization_barrier

    def to_owner(piece):
        piece = lax.all_to_all(piece, "x", split_axis=0, concat_axis=0, tiled=True)
        return piece.reshape(4 * depth, -1)

    joint = qkv_weight, qkv_grad, qkv_first, qkv_second
    own_one = to_owner(joint_adam(0, *joint))
    piece_two = joint_adam(1, *joint)
    normed = norm_rows(hidden_states, norm_gain)
    own_one, piece_two, normed = barrier((own_one, piece_two, normed))

    below_one, above_one = shift_z(own_one, 1), shift_z(own_one, -1)
    own_one_swapped = swap_cores(own_one)
    own_two = to_owner(piece_two)
    normed, own_two = barrier((normed, own_two))
    normed_rows = lax.all_to_all(normed, PLANE, split_axis=0, concat_axis=0, tiled=True)
    out_updated = adam_step(out_weight, out_grad, out_first, out_second)
    out_piece = out_updated.reshape(depth, 8, 4, 256).transpose(2, 0, 1, 3).reshape(4, depth, 2048)
    cosine, sine = rotary_tables(lengths)
    starts = piece_starts(4 * depth)
    below_one, above_one, own_two, own_one_swapped = barrier(
        (below_one, above_one, own_two, own_one_swapped)
    )
    far_one, above_two = shift_z(below_one, 1), shift_z(own_two, -1)
    above_one_swapped, below_one_swapped = swap_cores(above_one), swap_cores(below_one)
    own_two_swapped = swap_cores(own_two)
    far_one, above_two, own_two, above_one_swapped, below_one_swapped, own_two_swapped = barrier(
        (far_one, above_two, own_two, above_one_swapped, below_one_swapped, own_two_swapped)
    )
    normed_rows, out_piece, cosine, sine, starts = barrier(
        (normed_rows, out_piece, cosine, sine, starts)
    )
    out_own = to_owner(out_piece)

    rows = [normed_rows.reshape(-1, 2048)]
    pieces = both_cores(
        (0, 0, own_one, own_one_swapped),
        (1, 0, above_one, above_one_swapped),
        (3, 0, below_one, below_one_swapped),
        (2, 0, far_one, swap_cores(far_one)),
    )
    projected_one = product(rows, pieces, starts, 1, False, "qkv_partial_one")
    projected_one, own_two, above_two = barrier((projected_one, own_two, above_two))
    below_two, far_two = shift_z(own_two, 1), shift_z(above_two, -1)
    above_two_swapped = swap_cores(above_two)
    projected_one = projected_one.reshape(16, -1, 1280)
    fields_one = lax.all_to_all(projected_one, PLANE, split_axis=0, concat_axis=0, tiled=True)
    pieces = both_cores(
        (0, 0, own_two, own_two_swapped),
        (1, 0, above_two, above_two_swapped),
        (3, 0, below_two, swap_cores(below_two)),
        (2, 0, far_two, swap_cores(far_two)),
    )
    projected_two = product(rows, pieces, starts, 1, False, "qkv_partial_two")
    projected_two = projected_two.reshape(16, -1, 1280)
    projected_two, fields_one, out_own = barrier((projected_two, fields_one, out_own))
    out_below, out_above = shift_z(out_own, 1), shift_z(out_own, -1)
    out_own_swapped = swap_cores(out_own)
    fields_two = lax.all_to_all(projected_two, PLANE, split_axis=0, concat_axis=0, tiled=True)

    caches = rotated_key_cache, value_cache, lengths
    fields_shape = (16, PAIRS, 8, 1280)
    attended = attention(0, fields_one.reshape(fields_shape), cosine, sine, *caches)
    fields_two, attended, out_below, out_above, out_own_swapped = barrier(
        (fields_two, attended, out_below, out_above, out_own_swapped)
    )
    half = out_own.shape[0] // 2
    out_far = shift_z(out_below[:half], 1), shift_z(out_above[half:], -1)
    out_below_swapped, out_above_swapped = swap_cores(out_below), swap_cores(out_above)
    attended = attention(1, fields_two.reshape(fields_shape), cosine, sine, *caches, attended)
    attended, out_far, out_below_swapped, out_above_swapped = barrier(
        (attended, out_far, out_below_swapped, out_above_swapped)
    )
    attended = lax.all_to_all(attended, PLANE, split_axis=0, concat_axis=0, tiled=True)
    pieces = both_cores(
        (0, 0, out_own, out_own_swapped),
        (1, 0, out_above, out_above_swapped),
        (3, 0, out_below, out_below_swapped),
        (2, 0, out_far[0], swap_cores(out_far[0])),
        (2, half, out_far[1], swap_cores(out_far[1])),
    )
    rows = [attended.reshape(-1, 2048)]
    partial = product(rows, pieces, starts, 2, True, "out_partial")
    partial = lax.all_to_all(partial, ("y", "zh"), split_axis=0, concat_axis=0, tiled=True)
    total = jnp.sum(partial.reshape(4, 2, -1, 256).astype(jnp.float32), axis=0)
    total = total.astype(jnp.bfloat16).reshape(2, 4, 4, -1, DECODE_STEPS, 256)
    return total.transpose(4, 1, 0, 2, 3, 5).reshape(DECODE_STEPS, -1, 256)


def solution(mesh):
    every = ("zl", "c", "y", "zh", "x")
    fine = jax.sharding.Mesh(mesh.devices.reshape(2, 2, 4, 2, 4), every)
    return jax.shard_map(
        body,
        mesh=fine,
        in_specs=(
            P(None, every, None),
            P(),
            P(every),
            P(every, None, None),
            P(every, None, None),
        )
        + (P(every, None),) * 8,
        out_specs=P(None, ("zl", "c"), ("y", "zh", "x")),
        check_vma=False,
    )
```

```python
import functools
import math

import jax
import jax.numpy as jnp
from jax import lax
from jax.experimental import pallas as pl
from jax.experimental.pallas import tpu as pltpu
from jax.sharding import PartitionSpec as P

D = 8192
HQ = 64
KEY_HEADS = 8
HEAD_SIZE = 128
CONTEXT_SLOTS = 512
DECODE_STEPS = 4
QUERY_WIDTH = 8192
KEY_WIDTH = 1024


learn_rate = 0.008
beta_one = 0.9
beta_two = 0.95
bias_one = 1.0 - beta_one * beta_one
bias_two = 1.0 - beta_two * beta_two
adam_eps = 1e-08
decay_rate = 0.1
rope_base = 500000.0
norm_eps = 1e-05


def adam_step(weight, gradient, moment_one, moment_two):
    grad_wide = gradient.astype(jnp.float32)
    first_new = beta_one * moment_one.astype(jnp.float32) + (1.0 - beta_one) * grad_wide
    second_new = (
        beta_two * moment_two.astype(jnp.float32) + (1.0 - beta_two) * grad_wide * grad_wide
    )
    weight_wide = weight.astype(jnp.float32)
    update = (
        first_new / bias_one / (jnp.sqrt(second_new / bias_two) + adam_eps)
        + decay_rate * weight_wide
    )
    return (weight_wide - learn_rate * update).astype(jnp.bfloat16)


PAIRS = 3
Z_SIZE = 4
PLANE = ("y", "x")
VMEM_LIMIT = 56 * 1024 * 1024


def shift_z(value, step):
    def position(z):
        return (z % 2) * 2 + (z // 2) % 2

    return lax.ppermute(
        value, ("zl", "zh"), [(position(z), position(z + step + Z_SIZE)) for z in range(Z_SIZE)]
    )


def swap_cores(value):
    return lax.ppermute(value, "c", [(0, 1), (1, 0)])


def joint_adam_kernel(*refs):
    out_ref = refs[-1]
    query, key, value = (
        adam_step(*(ref[...] for ref in refs[part:12:3])) for part in range(3)
    )
    for x in range(2):
        out_ref[x, :, :1024] = query[:, x * 1024 : (x + 1) * 1024]
        out_ref[x, :, 1024:1152] = key[:, x * 128 : (x + 1) * 128]
        out_ref[x, :, 1152:] = value[:, x * 128 : (x + 1) * 128]


def joint_adam(half, *arrays):
    depth = arrays[0].shape[0]
    specs = [
        pl.BlockSpec((depth, 2048), lambda i: (0, 2 * half + i)),
        pl.BlockSpec((depth, 256), lambda i: (0, 32 + 2 * half + i)),
        pl.BlockSpec((depth, 256), lambda i: (0, 36 + 2 * half + i)),
    ]
    return pl.pallas_call(
        joint_adam_kernel,
        out_shape=jax.ShapeDtypeStruct((4, depth, 1280), jnp.bfloat16),
        grid=(2,),
        in_specs=specs * 4,
        out_specs=pl.BlockSpec((2, depth, 1280), lambda i: (i, 0, 0)),
        compiler_params=pltpu.CompilerParams(vmem_limit_bytes=VMEM_LIMIT),
        name="joint_adam",
    )(*(array for array in arrays for _ in range(3)))


def norm_kernel(hidden_ref, gain_ref, out_ref, scratch_ref):
    gain = gain_ref[...].astype(jnp.float32)
    rows = hidden_ref.shape[1]
    for step in range(DECODE_STEPS):
        wide = hidden_ref[step].astype(jnp.float32)
        inverse = lax.rsqrt(jnp.mean(wide * wide, axis=-1, keepdims=True) + norm_eps)
        normed = wide * inverse * gain
        for row in range(rows):
            at = row * DECODE_STEPS + step
            scratch_ref[at : at + 1, :] = normed[row : row + 1]
    for natural in range(D // 256):
        start = ((natural >> 3) * 2 + (natural & 1)) * 256
        block = scratch_ref[:, natural * 256 : (natural + 1) * 256].astype(jnp.bfloat16)
        for x in range(4):
            out_ref[4 * ((natural >> 1) & 3) + x, :, start : start + 256] = block


def norm_rows(hidden_states, norm_gain):
    rows = DECODE_STEPS * hidden_states.shape[1]
    vmem = pl.BlockSpec(memory_space=pltpu.VMEM)
    return pl.pallas_call(
        norm_kernel,
        out_shape=jax.ShapeDtypeStruct((16, rows, D // 4), jnp.bfloat16),
        in_specs=[vmem, vmem],
        out_specs=vmem,
        scratch_shapes=[pltpu.VMEM((rows, D), jnp.float32)],
        compiler_params=pltpu.CompilerParams(vmem_limit_bytes=16 * 1024 * 1024),
        name="norm_rows",
    )(hidden_states, norm_gain[None])


def rotary_tables(lengths):
    half_width = HEAD_SIZE // 2
    frequency = jnp.power(
        rope_base, -2.0 * jnp.arange(half_width, dtype=jnp.float32) / HEAD_SIZE
    )
    positions = lengths[:, None] + jnp.arange(DECODE_STEPS, dtype=jnp.int32)[None, :]
    angles = positions.astype(jnp.float32)[..., None] * frequency
    cosine, sine = jnp.cos(angles), jnp.sin(angles)
    shape = (PAIRS, 8, HEAD_SIZE)
    return (
        jnp.concatenate([cosine, cosine], axis=-1).reshape(shape),
        jnp.concatenate([-sine, sine], axis=-1).reshape(shape),
    )


def attention_kernel(
    lengths_ref, field_ref, cos_ref, sin_ref, key_ref, value_ref, *refs
):
    out_ref = refs[-1]
    pair = pl.program_id(0)
    cosine, sine = cos_ref[0], sin_ref[0]
    scale = 1.0 / math.sqrt(HEAD_SIZE)
    line = lax.broadcasted_iota(jnp.int32, (128, 1), 0)
    second_row = ((line >> 2) & 1) == 1
    step = line & 3
    length = jnp.where(second_row, lengths_ref[2 * pair + 1], lengths_ref[2 * pair])
    live = lax.broadcasted_iota(jnp.int32, (128, CONTEXT_SLOTS), 1) < length
    fresh_column = lax.broadcasted_iota(jnp.int32, (128, 8), 1)
    fresh_live = (((fresh_column >> 2) & 1) == ((line >> 2) & 1)) & ((fresh_column & 3) <= step)

    def field(x, start):
        total = None
        for y in range(4):
            term = field_ref[4 * y + x, 0, :, start : start + 128].astype(jnp.float32)
            total = term if total is None else total + term
        return total.astype(jnp.bfloat16).astype(jnp.float32)

    def rotate(vector):
        return vector * cosine + pltpu.roll(vector, 64, 1) * sine

    def times_transposed(left, right):
        return lax.dot_general(
            left, right, (((1,), (1,)), ((), ())), preferred_element_type=jnp.float32
        )

    for first in range(0, KEY_HEADS // 2, 2):
        cached, fresh, fresh_values = [], [], []
        for kv in (first, first + 1):
            columns = slice(kv * HEAD_SIZE, (kv + 1) * HEAD_SIZE)
            query = jnp.concatenate(
                [rotate(field(kv, h * 128)) for h in range(8)], axis=0
            ).astype(jnp.bfloat16)
            fresh_key = rotate(field(kv, 1024)).astype(jnp.bfloat16)
            fresh_values.append(field(kv, 1152))
            cached.append(
                jnp.where(
                    second_row[:64],
                    times_transposed(query, key_ref[1, :, columns]),
                    times_transposed(query, key_ref[0, :, columns]),
                )
            )
            fresh.append(times_transposed(query, fresh_key))
        scores = jnp.where(live, jnp.concatenate(cached, axis=0) * scale, -jnp.inf)
        fresh_scores = jnp.where(fresh_live, jnp.concatenate(fresh, axis=0) * scale, -jnp.inf)
        highest = jnp.maximum(
            jnp.max(scores, axis=-1, keepdims=True), jnp.max(fresh_scores, axis=-1, keepdims=True)
        )
        weight = jnp.exp(scores - highest)
        fresh_weight = jnp.exp(fresh_scores - highest)
        inverse = 1.0 / (
            jnp.sum(weight, axis=-1, keepdims=True) + jnp.sum(fresh_weight, axis=-1, keepdims=True)
        )
        prob = weight * inverse
        fresh_prob = (fresh_weight * inverse).astype(jnp.bfloat16)
        columns = slice(first * 128, first * 128 + 256)
        attended = (
            jnp.dot(
                jnp.where(second_row, 0.0, prob).astype(jnp.bfloat16),
                value_ref[0, :, columns],
                preferred_element_type=jnp.float32,
            )
            + jnp.dot(
                jnp.where(second_row, prob, 0.0).astype(jnp.bfloat16),
                value_ref[1, :, columns],
                preferred_element_type=jnp.float32,
            )
            + jnp.dot(
                fresh_prob,
                jnp.concatenate(fresh_values, axis=1).astype(jnp.bfloat16),
                preferred_element_type=jnp.float32,
            )
        )
        for h in range(0, 16, 2):
            natural = 4 * first + h // 2
            y = (natural >> 1) & 3
            start = ((natural >> 3) * 2 + (natural & 1)) * 256
            side = slice(128 * (h // 8), 128 * (h // 8) + 128)
            block = jnp.concatenate(
                [attended[8 * h : 8 * h + 8, side], attended[8 * h + 8 : 8 * h + 16, side]], axis=1
            ).astype(jnp.bfloat16)
            for copy in range(4):
                out_ref[4 * y + copy, 0, :, start : start + 256] = block


def attention(half, fields, cosine, sine, keys, values, lengths, *before):
    table = pl.BlockSpec((1, 8, HEAD_SIZE), lambda i, *_: (i, 0, 0))
    cache = pl.BlockSpec((2, CONTEXT_SLOTS, KEY_WIDTH // 2), lambda i, *_: (i, 0, half))
    return pl.pallas_call(
        attention_kernel,
        out_shape=jax.ShapeDtypeStruct((16, PAIRS, 8, 2048), jnp.bfloat16),
        grid_spec=pltpu.PrefetchScalarGridSpec(
            num_scalar_prefetch=1,
            grid=(PAIRS,),
            in_specs=[
                pl.BlockSpec((16, 1, 8, 1280), lambda i, *_: (0, i, 0, 0)),
                table,
                table,
                cache,
                cache,
            ]
            + [pl.BlockSpec(memory_space=pl.ANY)] * len(before),
            out_specs=pl.BlockSpec((16, 1, 8, 1024), lambda i, *_: (0, i, 0, half)),
        ),
        input_output_aliases={6: 0} if before else {},
        compiler_params=pltpu.CompilerParams(vmem_limit_bytes=VMEM_LIMIT),
        cost_estimate=pl.CostEstimate(
            flops=PAIRS * 4 * 8 * 64 * 512 * 128,
            bytes_accessed=PAIRS * 2 * 1024 * 1024,
            transcendentals=PAIRS * 4 * 64 * 512,
        ),
        name="attention",
    )(lengths, fields, cosine, sine, keys, values, *before)


def product_kernel(parts, places, by_block, start_ref, *refs):
    rows, pieces = refs[:parts], refs[parts : parts + len(places)]
    out_ref, rows_held, held, row_sems, piece_sems = refs[parts + len(places) :]
    width = rows[0].shape[1]
    row_copies = [
        pltpu.make_async_copy(part, rows_held.at[:, pl.ds(i * width, width)], row_sems.at[i])
        for i, part in enumerate(rows)
    ]
    for copy in row_copies:
        copy.start()

    blocks, columns = held.shape[0], held.shape[2]

    def copies(block):
        for i, (piece, (index, offset)) in enumerate(zip(pieces, places)):
            start = pl.multiple_of(start_ref[index] + offset, 128)
            yield pltpu.make_async_copy(
                piece.at[:, pl.ds(block * columns, columns)],
                held.at[block, pl.ds(start, piece.shape[0]), :],
                piece_sems.at[block, i],
            )

    for block in range(blocks):
        for copy in copies(block):
            copy.start()
    for copy in row_copies:
        copy.wait()
    for block in range(blocks):
        for copy in copies(block):
            copy.wait()
        for part in range(columns // 256):
            result = jnp.dot(
                rows_held[...],
                held[block, :, part * 256 : (part + 1) * 256],
                preferred_element_type=jnp.float32,
            ).astype(jnp.bfloat16)
            at = block * (columns // 256) + part
            if by_block:
                out_ref[at] = result
            else:
                out_ref[:, at * 256 : (at + 1) * 256] = result


def product(rows, pieces, starts, turns, by_block, name):
    places = tuple(place for place, _ in pieces)
    weights = [weight for _, weight in pieces]
    count, depth = rows[0].shape[0], sum(part.shape[1] for part in rows)
    columns = weights[0].shape[1]
    blocks = columns // 256
    anywhere = pl.BlockSpec(memory_space=pl.ANY)
    return pl.pallas_call(
        functools.partial(product_kernel, len(rows), places, by_block),
        out_shape=jax.ShapeDtypeStruct(
            (blocks, count, 256) if by_block else (count, columns), jnp.bfloat16
        ),
        in_specs=[pl.BlockSpec(memory_space=pltpu.SMEM)] + [anywhere] * (len(rows) + len(weights)),
        out_specs=pl.BlockSpec(memory_space=pltpu.VMEM),
        scratch_shapes=[
            pltpu.VMEM((count, depth), jnp.bfloat16),
            pltpu.VMEM((turns, depth, columns // turns), jnp.bfloat16),
            pltpu.SemaphoreType.DMA((len(rows),)),
            pltpu.SemaphoreType.DMA((turns, len(weights))),
        ],
        compiler_params=pltpu.CompilerParams(vmem_limit_bytes=VMEM_LIMIT),
        cost_estimate=pl.CostEstimate(
            flops=2 * count * depth * columns,
            bytes_accessed=2 * depth * (count + columns),
            transcendentals=0,
        ),
        name=name,
    )(starts, *rows, *weights)


def piece_starts(size):
    ahead = jnp.arange(8, dtype=jnp.int32)
    plane = (lax.axis_index("zh") * 2 + lax.axis_index("zl") + (ahead >> 1)) & 3
    core = (lax.axis_index("c") + ahead) & 1
    return ((plane & 1) * 4 + core * 2 + (plane >> 1)) * size


def both_cores(*pieces):
    result = []
    for plane, offset, own, other in pieces:
        result += [((2 * plane, offset), own), ((2 * plane + 1, offset), other)]
    return result


def body(
    hidden_states,
    norm_gain,
    lengths,
    rotated_key_cache,
    value_cache,
    qkv_weight,
    qkv_grad,
    qkv_first,
    qkv_second,
    out_weight,
    out_grad,
    out_first,
    out_second,
):
    depth = qkv_weight.shape[0]
    barrier = lax.optimization_barrier

    def to_owner(piece):
        piece = lax.all_to_all(piece, "x", split_axis=0, concat_axis=0, tiled=True)
        return piece.reshape(4 * depth, -1)

    joint = qkv_weight, qkv_grad, qkv_first, qkv_second
    own_one = to_owner(joint_adam(0, *joint))
    piece_two = joint_adam(1, *joint)
    normed = norm_rows(hidden_states, norm_gain)
    own_one, piece_two, normed = barrier((own_one, piece_two, normed))

    below_one, above_one = shift_z(own_one, 1), shift_z(own_one, -1)
    own_one_swapped = swap_cores(own_one)
    own_two = to_owner(piece_two)
    normed, own_two = barrier((normed, own_two))
    normed_rows = lax.all_to_all(normed, PLANE, split_axis=0, concat_axis=0, tiled=True)
    out_updated = adam_step(out_weight, out_grad, out_first, out_second)
    out_piece = out_updated.reshape(depth, 8, 4, 256).transpose(2, 0, 1, 3).reshape(4, depth, 2048)
    cosine, sine = rotary_tables(lengths)
    starts = piece_starts(4 * depth)
    below_one, above_one, own_two, own_one_swapped = barrier(
        (below_one, above_one, own_two, own_one_swapped)
    )
    far_one, above_two = shift_z(below_one, 1), shift_z(own_two, -1)
    above_one_swapped, below_one_swapped = swap_cores(above_one), swap_cores(below_one)
    own_two_swapped = swap_cores(own_two)
    far_one, above_two, own_two, above_one_swapped, below_one_swapped, own_two_swapped = barrier(
        (far_one, above_two, own_two, above_one_swapped, below_one_swapped, own_two_swapped)
    )
    normed_rows, out_piece, cosine, sine, starts = barrier(
        (normed_rows, out_piece, cosine, sine, starts)
    )
    out_own = to_owner(out_piece)

    rows = [normed_rows.reshape(-1, 2048)]
    pieces = both_cores(
        (0, 0, own_one, own_one_swapped),
        (1, 0, above_one, above_one_swapped),
        (3, 0, below_one, below_one_swapped),
        (2, 0, far_one, swap_cores(far_one)),
    )
    projected_one = product(rows, pieces, starts, 1, False, "qkv_partial_one")
    projected_one, own_two, above_two = barrier((projected_one, own_two, above_two))
    below_two, far_two = shift_z(own_two, 1), shift_z(above_two, -1)
    above_two_swapped = swap_cores(above_two)
    projected_one = projected_one.reshape(16, -1, 1280)
    fields_one = lax.all_to_all(projected_one, PLANE, split_axis=0, concat_axis=0, tiled=True)
    pieces = both_cores(
        (0, 0, own_two, own_two_swapped),
        (1, 0, above_two, above_two_swapped),
        (3, 0, below_two, swap_cores(below_two)),
        (2, 0, far_two, swap_cores(far_two)),
    )
    projected_two = product(rows, pieces, starts, 1, False, "qkv_partial_two")
    projected_two = projected_two.reshape(16, -1, 1280)
    projected_two, fields_one, out_own = barrier((projected_two, fields_one, out_own))
    out_below, out_above = shift_z(out_own, 1), shift_z(out_own, -1)
    out_own_swapped = swap_cores(out_own)
    fields_two = lax.all_to_all(projected_two, PLANE, split_axis=0, concat_axis=0, tiled=True)

    caches = rotated_key_cache, value_cache, lengths
    fields_shape = (16, PAIRS, 8, 1280)
    attended = attention(0, fields_one.reshape(fields_shape), cosine, sine, *caches)
    fields_two, attended, out_below, out_above, out_own_swapped = barrier(
        (fields_two, attended, out_below, out_above, out_own_swapped)
    )
    half = out_own.shape[0] // 2
    out_far = shift_z(out_below[:half], 1), shift_z(out_above[half:], -1)
    out_below_swapped, out_above_swapped = swap_cores(out_below), swap_cores(out_above)
    attended = attention(1, fields_two.reshape(fields_shape), cosine, sine, *caches, attended)
    attended = lax.all_to_all(attended, PLANE, split_axis=0, concat_axis=0, tiled=True)
    pieces = both_cores(
        (0, 0, out_own, out_own_swapped),
        (1, 0, out_above, out_above_swapped),
        (3, 0, out_below, out_below_swapped),
        (2, 0, out_far[0], swap_cores(out_far[0])),
        (2, half, out_far[1], swap_cores(out_far[1])),
    )
    rows = [attended.reshape(-1, 2048)]
    partial = product(rows, pieces, starts, 2, True, "out_partial")
    partial = lax.all_to_all(partial, ("y", "zh"), split_axis=0, concat_axis=0, tiled=True)
    total = jnp.sum(partial.reshape(4, 2, -1, 256).astype(jnp.float32), axis=0)
    total = total.astype(jnp.bfloat16).reshape(2, 4, 4, -1, DECODE_STEPS, 256)
    return total.transpose(4, 1, 0, 2, 3, 5).reshape(DECODE_STEPS, -1, 256)


def solution(mesh):
    every = ("zl", "c", "y", "zh", "x")
    fine = jax.sharding.Mesh(mesh.devices.reshape(2, 2, 4, 2, 4), every)
    return jax.shard_map(
        body,
        mesh=fine,
        in_specs=(
            P(None, every, None),
            P(),
            P(every),
            P(every, None, None),
            P(every, None, None),
        )
        + (P(every, None),) * 8,
        out_specs=P(None, ("zl", "c"), ("y", "zh", "x")),
        check_vma=False,
    )
```
